256 devices in a mesh: elem: 16 (over z, core), four: 16 (over y, x).
Axes of the slice: x: 4, y: 4, z: 8, core: 2. Of those that a mesh axis runs over, the one named last changes fastest.
Arguments:
- vel_hat: float32 [3, 512, 32768], P(None, 'four', 'elem')
- metric: float32 [4, 512], P(None, 'elem'), may hold values from -0.4 to 0.4
- area: float32 [512], P('elem'), may hold values from 0.5 to 2
- visc: float32 [32768], P('elem'), may hold values from 0.05 to 0.5
- rotor_element: int32 [512], P('elem'), may hold values from 0 to 31
- stator_element: int32 [512], P('elem'), may hold values from 0 to 31
- mortar_offset: int32 [512], P('elem'), may hold values from 0 to 7
- stator_source: int32 [512], P('elem'), may hold values from 0 to 511, as said below
Outputs:
- tendency: float32 [3, 512, 32768], P(None, 'four', 'elem')
The draws below stay inside these ranges and needn't reach their ends.
Inputs may be any that keep to these rules, and one draw needn't show every extreme that they name: stator_source[g] is d * 32 + s for a slot s of elem index d.
All inputs are finite; a program needn't handle non-finite values.
Results may differ from the reference program's by a relative error of at most 0.0001.
Values sent between devices are 32-bit elements; how exact they have to be, the bound alone decides.
No kernel may reach another device: no remote copies, remote signals or barrier semaphores. Data moves between devices by JAX's collectives and lax.ppermute only.
A program may use at most 128 MiB of HBM per device.

```python
import math
import jax
import jax.numpy as jnp
import numpy as np
from jax import lax

NQ = 8
MODES = 512
PLANES = 768
E_DEV = 32
R_DEV = 32
CAP = 32
ELEMS = 512
NODES = 32768
ROTOR = 512
STATOR = 512
N_ELEM = 16
N_FOUR = 16


def draw_vel_hat(key, part):
    key = jax.random.fold_in(key, 11)
    column = jnp.arange(MODES, dtype=jnp.int32)
    number = jnp.where(column == 1, MODES // 2, column // 2)
    amplitude = 0.125 / (1.0 + number.astype(jnp.float32) / 32.0)
    base = jax.random.normal(key, (3, MODES, NODES), jnp.float32)
    return (base * amplitude[None, :, None]).astype(jnp.float32)


def draw_stator_source(key, part):
    key = jax.random.fold_in(key, 23)
    key_len = jax.random.fold_in(key, 0)
    key_pick = jax.random.fold_in(key, 2)
    lengths = jax.random.randint(key_len, (N_ELEM,), 1, R_DEV + 1)
    favored = N_ELEM - 1
    lengths = jnp.where(jnp.arange(N_ELEM) == favored, R_DEV, lengths).astype(jnp.int32)
    ends = jnp.cumsum(lengths)
    starts = ends - lengths
    circuit = ends[-1]
    slot_ids = jnp.arange(N_ELEM * CAP, dtype=jnp.int32)
    spread_ids = slot_ids % CAP * N_ELEM + slot_ids // CAP
    spaced = spread_ids * circuit // (N_ELEM * CAP)
    anchor = jax.random.randint(key_pick, (), 0, N_ELEM * CAP)
    target_end = starts[favored] + R_DEV - 1
    rotation = (target_end - spaced[anchor]) % circuit
    position = (spaced + rotation) % circuit
    position = jnp.where(slot_ids == (anchor + 1) % (N_ELEM * CAP), 0, position)
    owner = jnp.sum((ends[None, :] <= position[:, None]).astype(jnp.int32), axis=1)
    within = position - starts[owner]
    return (owner * R_DEV + within).astype(jnp.int32)


def plant(values, rng, smallest, top_value):
    extent = values.shape
    place = [jax.random.randint(jax.random.fold_in(rng, axis), (), 0, extent[axis]) for axis in range(len(extent))]
    values = values.at[tuple(place)].set(smallest)
    longest = extent.index(max(extent))
    place[longest] = (place[longest] + 1) % extent[longest]
    return values.at[tuple(place)].set(top_value)


def steps_of(stream_key, dims, cuts, smallest, top_value):
    loudness = 1.0
    for dim, shards_of in cuts:
        heights = jax.random.uniform(jax.random.fold_in(jax.random.fold_in(stream_key, 6), dim), (shards_of,), jnp.float32, smallest / len(cuts), top_value / len(cuts))
        loudness = loudness * jnp.repeat(jnp.exp(heights), dims[dim] // shards_of).reshape((-1,) + (1,) * (len(dims) - 1 - dim))
    return loudness


def bell_draw(own_key, shape, scale, limit, pieces=(), held_as=jnp.bfloat16):
    values = jax.random.normal(own_key, shape, jnp.float32) * scale
    if len(pieces) > 0:
        values = steps_of(own_key, shape, pieces, -0.22, 0.18) * values
    return jnp.clip(values, min=-limit, max=limit).astype(held_as)


def setup_inputs(seed: int = 0) -> dict:
    key_of = jax.random.split(jax.random.key(seed), 9)
    vel_hat = draw_vel_hat(jax.random.fold_in(key_of[8], 71), 0)
    metric = bell_draw(key_of[1], (4, ELEMS), 0.1, 0.4, ((1, 16),), jnp.float32)
    area = jnp.clip(jnp.exp(math.log(2.0) - 1.3862944 * jax.random.uniform(key_of[2], (ELEMS,), jnp.float32) ** steps_of(key_of[2], (ELEMS,), ((0, 16),), -0.2, 0.2)), 0.5, 2.0)
    visc = jnp.clip(jnp.exp(math.log(0.5) - 2.3025851 * jax.random.uniform(key_of[3], (NODES,), jnp.float32) ** steps_of(key_of[3], (NODES,), ((0, 16),), -0.2, 0.2)), 0.05, 0.5)
    rotor_element = plant(jax.random.randint(key_of[4], (ROTOR,), 0, E_DEV), jax.random.fold_in(key_of[4], 1), 0, E_DEV - 1).astype(jnp.int32)
    stator_element = plant(jax.random.randint(key_of[5], (STATOR,), 0, E_DEV), jax.random.fold_in(key_of[5], 1), 0, E_DEV - 1).astype(jnp.int32)
    mortar_offset = plant(jax.random.randint(key_of[6], (STATOR,), 0, NQ), jax.random.fold_in(key_of[6], 1), 0, NQ - 1).astype(jnp.int32)
    stator_source = draw_stator_source(jax.random.fold_in(key_of[8], 71), 0)
    return dict(vel_hat=vel_hat, metric=metric, area=area, visc=visc, rotor_element=rotor_element, stator_element=stator_element, mortar_offset=mortar_offset, stator_source=stator_source)


HIGHEST = lax.Precision.HIGHEST
LAMBDA_COEF = 10.0
TAU_COEF = 2.0
KZ_DIV = 32.0


def element_tables():
    order = NQ - 1
    points = -np.cos(np.pi * np.arange(NQ) / order)
    barycentric = np.array([(-1.0) ** index_a for index_a in range(NQ)])
    barycentric[0] *= 0.5
    barycentric[-1] *= 0.5
    derivative = np.zeros((NQ, NQ))
    for index_a in range(NQ):
        for index_b in range(NQ):
            if index_a != index_b:
                derivative[index_a, index_b] = barycentric[index_b] / barycentric[index_a] / (points[index_a] - points[index_b])
        derivative[index_a, index_a] = -np.sum(derivative[index_a])
    angles = np.pi * np.arange(NQ) / order
    weights = np.ones(NQ)
    for harmonic in range(1, order // 2 + 1):
        factor = 1.0 if 2 * harmonic == order else 2.0
        weights = weights - factor * np.cos(2 * harmonic * angles) / (4 * harmonic * harmonic - 1)
    weights = weights * 2.0 / order
    weights[0] *= 0.5
    weights[-1] *= 0.5
    identity = np.eye(NQ)
    along_xi = np.kron(np.eye(2), np.kron(identity, derivative))
    along_eta = np.kron(np.eye(2), np.kron(derivative, identity))
    node_weight = np.kron(weights, weights)
    interp = np.ones((NQ, NQ, NQ))
    for offset in range(NQ):
        targets = points * (1.0 - offset / 16.0) + offset / 16.0
        for index_a in range(NQ):
            for index_b in range(NQ):
                for index_c in range(NQ):
                    if index_c != index_b:
                        interp[offset, index_a, index_b] *= (targets[index_a] - points[index_c]) / (points[index_b] - points[index_c])
    return (jnp.asarray(along_xi, jnp.float32), jnp.asarray(along_eta, jnp.float32),
            jnp.asarray(node_weight, jnp.float32), jnp.asarray(interp, jnp.float32))


def wavenumbers():
    column = jnp.arange(MODES, dtype=jnp.int32)
    number = jnp.where(column == 1, MODES // 2, column // 2)
    return number.astype(jnp.float32) / KZ_DIV


def spectral_tables():
    column = jnp.arange(MODES, dtype=jnp.int32)
    number = jnp.where(column == 1, MODES // 2, column // 2)
    plane = jnp.arange(PLANES, dtype=jnp.int32)
    phase = (plane[:, None] * number[None, :]) % PLANES
    angle = phase.astype(jnp.float32) * (2.0 * math.pi / PLANES)
    sine_part = (column % 2 == 1) & (column > 1)
    wave = number.astype(jnp.float32) / KZ_DIV
    synthesis = jnp.where(sine_part[None, :], jnp.sin(angle), jnp.cos(angle))
    slope = jnp.where(sine_part[None, :], wave[None, :] * jnp.cos(angle), -wave[None, :] * jnp.sin(angle))
    slope = jnp.where(column[None, :] == 1, jnp.float32(0.0), slope)
    scaling = jnp.where(column == 0, 1.0 / PLANES, 2.0 / PLANES).astype(jnp.float32)
    analysis = synthesis.T * scaling[:, None]
    return synthesis, slope, analysis


def apply_block(field, table, forward):
    shape = field.shape
    width = 2 * NQ * NQ
    blocks = field.reshape(shape[:-2] + (shape[-2] * shape[-1] // width, width))
    if forward:
        result = jnp.einsum('...n,kn->...k', blocks, table, precision=HIGHEST)
    else:
        result = jnp.einsum('...n,nk->...k', blocks, table, precision=HIGHEST)
    return result.reshape(shape)


def raw_grads(field, tables):
    shape = field.shape
    grid = field.reshape(shape[:-1] + (shape[-1] // (NQ * NQ), NQ * NQ))
    return apply_block(grid, tables[0], True), apply_block(grid, tables[1], True)


def plane_gradients(field, metric, tables):
    grad_xi, grad_eta = raw_grads(field, tables)
    grad_x = metric[0][:, None] * grad_xi + metric[2][:, None] * grad_eta
    grad_y = metric[1][:, None] * grad_xi + metric[3][:, None] * grad_eta
    return grad_x.reshape(field.shape), grad_y.reshape(field.shape)


def helmholtz(field, metric, area, visc, wave_sq, tables):
    shape = field.shape
    elements = shape[-1] // (NQ * NQ)
    grad_xi, grad_eta = raw_grads(field, tables)
    grad_x = metric[0][:, None] * grad_xi + metric[2][:, None] * grad_eta
    grad_y = metric[1][:, None] * grad_xi + metric[3][:, None] * grad_eta
    weight = area[:, None] * tables[2][None, :]
    viscous = visc.reshape(elements, NQ * NQ)
    flux_x = weight * viscous * grad_x
    flux_y = weight * viscous * grad_y
    back_xi = metric[0][:, None] * flux_x + metric[1][:, None] * flux_y
    back_eta = metric[2][:, None] * flux_x + metric[3][:, None] * flux_y
    stiff = apply_block(back_xi, tables[0], False) + apply_block(back_eta, tables[1], False)
    grid = field.reshape(shape[:-1] + (elements, NQ * NQ))
    mass = weight * (LAMBDA_COEF + viscous * wave_sq[:, None, None]) * grid
    return (mass + stiff).reshape(shape)


def modal_dz(field, first_pair):
    shape = field.shape
    pairs = field.reshape(shape[0], shape[1] // 2, 2, shape[2])
    wave = (first_pair + jnp.arange(shape[1] // 2, dtype=jnp.int32)).astype(jnp.float32) / KZ_DIV
    cos_new = wave[:, None] * pairs[:, :, 1]
    sin_new = -wave[:, None] * pairs[:, :, 0]
    return jnp.stack([cos_new, sin_new], 2).reshape(shape)


def advect_from_gradients(bundle, synthesis, analysis):
    velocity = jnp.einsum('qm,cmp->cqp', synthesis, bundle[0:3], precision=HIGHEST)
    results = []
    for component in range(3):
        along_x = jnp.dot(synthesis, bundle[3 + component], precision=HIGHEST)
        along_y = jnp.dot(synthesis, bundle[6 + component], precision=HIGHEST)
        along_z = jnp.dot(synthesis, bundle[9 + component], precision=HIGHEST)
        advect = velocity[0] * along_x + velocity[1] * along_y + velocity[2] * along_z
        results.append(jnp.dot(analysis, advect, precision=HIGHEST))
    return jnp.stack(results, 0)


def reference(vel_hat, metric, area, visc, rotor_element, stator_element, mortar_offset, stator_source):
    tables = element_tables()
    synthesis, slope, analysis = spectral_tables()
    wave = wavenumbers()
    span_count = E_DEV // N_FOUR
    block_count = ELEMS // span_count
    width = span_count * NQ * NQ
    blocks = vel_hat.reshape(3, MODES, block_count, width).transpose(2, 0, 1, 3)
    metric_blocks = metric.reshape(4, block_count, span_count).transpose(1, 0, 2)
    area_blocks = area.reshape(block_count, span_count)
    visc_blocks = visc.reshape(block_count, width)

    def one_block(packed):
        field, geometry, sizes_here, viscous = packed
        helm = helmholtz(field, geometry, sizes_here, viscous, wave * wave, tables)
        grad_x, grad_y = plane_gradients(field, geometry, tables)
        grad_z = modal_dz(field, jnp.int32(0))
        bundle = jnp.concatenate([field, grad_x, grad_y, grad_z], 0)
        nonlinear = advect_from_gradients(bundle, synthesis, analysis)
        return -nonlinear - helm

    outputs = lax.map(one_block, (blocks, metric_blocks, area_blocks, visc_blocks))
    local_part = outputs.transpose(1, 2, 0, 3).reshape(3, MODES, NODES)

    grid = vel_hat.reshape(3, MODES, ELEMS, NQ * NQ)
    rotor_owner = jnp.arange(ROTOR, dtype=jnp.int32) // R_DEV * E_DEV + rotor_element
    traces = grid[:, :, rotor_owner, NQ * NQ - NQ:]
    received = traces[:, :, stator_source]
    onehot = (mortar_offset[:, None] == jnp.arange(NQ, dtype=jnp.int32)[None, :]).astype(jnp.float32)
    matrices = jnp.einsum('co,oji->cji', onehot, tables[3], precision=HIGHEST)
    mortar = jnp.einsum('cji,abci->abcj', matrices, received, precision=HIGHEST)
    stator_owner = jnp.arange(STATOR, dtype=jnp.int32) // CAP * E_DEV + stator_element
    own = grid[:, :, stator_owner, :NQ]
    penalty = TAU_COEF * (mortar - own)
    bottom = jnp.zeros((3, MODES, ELEMS, NQ), jnp.float32).at[:, :, stator_owner, :].add(penalty)
    filled = jnp.concatenate([bottom, jnp.zeros((3, MODES, ELEMS, NQ * NQ - NQ), jnp.float32)], -1)
    return local_part + filled.reshape(3, MODES, NODES)
```

```python
import math

import jax
import jax.numpy as jnp
import numpy as np
from jax import lax
from jax.experimental import pallas as pl
from jax.experimental.pallas import tpu as pltpu
from jax.sharding import PartitionSpec as P

NQ = 8
MODES = 512
PLANES = 768
HALF = PLANES // 2
PAIRS = MODES // 2
GROUPS = 16
ROWS = 96
LANES = 128

LAMBDA_COEF = 10.0
TAU_COEF = 2.0
KZ_DIV = 32.0

F32 = jnp.float32
BF16 = jnp.bfloat16
VMEM = pltpu.MemorySpace.VMEM
SMEM = pltpu.MemorySpace.SMEM


def element_tables():
    order = NQ - 1
    points = -np.cos(np.pi * np.arange(NQ) / order)
    barycentric = np.array([(-1.0) ** index_a for index_a in range(NQ)])
    barycentric[0] *= 0.5
    barycentric[-1] *= 0.5
    derivative = np.zeros((NQ, NQ))
    for index_a in range(NQ):
        for index_b in range(NQ):
            if index_a != index_b:
                derivative[index_a, index_b] = (
                    barycentric[index_b]
                    / barycentric[index_a]
                    / (points[index_a] - points[index_b])
                )
        derivative[index_a, index_a] = -np.sum(derivative[index_a])
    angles = np.pi * np.arange(NQ) / order
    weights = np.ones(NQ)
    for harmonic in range(1, order // 2 + 1):
        weights = weights - 2.0 * np.cos(2 * harmonic * angles) / (4 * harmonic * harmonic - 1)
    weights = weights * 2.0 / order
    weights[0] *= 0.5
    weights[-1] *= 0.5
    identity = np.eye(NQ)
    along_xi = np.kron(np.eye(2), np.kron(identity, derivative))
    along_eta = np.kron(np.eye(2), np.kron(derivative, identity))
    node_weight = np.kron(weights, weights)
    interp = np.ones((NQ, NQ, NQ))
    for offset in range(NQ):
        targets = points * (1.0 - offset / 16.0) + offset / 16.0
        for index_a in range(NQ):
            for index_b in range(NQ):
                for index_c in range(NQ):
                    if index_c != index_b:
                        interp[offset, index_a, index_b] *= (targets[index_a] - points[index_c]) / (
                            points[index_b] - points[index_c]
                        )
    return along_xi, along_eta, node_weight, interp


def two_parts(table):
    table = np.asarray(table, np.float32)
    high = table.astype(BF16)
    low = (table - high.astype(np.float32)).astype(BF16)
    return high, low


def as_left(table):
    high, low = two_parts(table)
    return jnp.asarray(np.concatenate([high, low, high], 1))


def as_right(table):
    high, low = two_parts(table)
    return jnp.asarray(np.concatenate([high, low, high], 0))


def span_tables():
    plane = np.arange(HALF)[:, None]
    number = np.arange(PAIRS)[None, :]
    angle = 2.0 * np.pi * ((plane * number) % PLANES) / PLANES
    cosine, sine = np.cos(angle), np.sin(angle)
    scale = np.full((PAIRS, 1), 2.0 / PLANES)
    scale[0] = 1.0 / PLANES
    return cosine, sine, cosine.T * scale, sine.T * (2.0 / PLANES)


def split(value):
    high = value.astype(BF16)
    low = (value - high.astype(F32)).astype(BF16)
    return high, low


def dot(left, right):
    return jnp.dot(left, right, preferred_element_type=F32)


def left_split(value):
    high, low = split(value)
    return jnp.concatenate([high, high, low], -1)


def right_split(value):
    high, low = split(value)
    return jnp.concatenate([high, high, low], 0)


def lane_scalars(first, second):
    lane = lax.broadcasted_iota(jnp.int32, (1, LANES), 1)
    return jnp.where(lane < LANES // 2, first, second)


def pack_kernel(field_ref, out_ref, in_ref, done_ref, in_sems, out_sems):
    def load(block):
        return pltpu.make_async_copy(
            field_ref.at[:, pl.ds(block * LANES, LANES)], in_ref.at[block], in_sems.at[block]
        )

    def store(block):
        return pltpu.make_async_copy(done_ref.at[block], out_ref.at[block], out_sems.at[block])

    for block in range(GROUPS):
        load(block).start()
    for block in range(GROUPS):
        load(block).wait()
        for component in range(3):
            for parity in range(2):
                done_ref[block, pl.ds(component * 32 + parity * 16, 16), :] = in_ref[
                    block, pl.ds(component * 32 + parity, 16, stride=2), :
                ]
        store(block).start()
    for block in range(GROUPS):
        store(block).wait()


def pack(field):
    anywhere = pl.BlockSpec(memory_space=pl.ANY)
    return pl.pallas_call(
        pack_kernel,
        in_specs=[anywhere],
        out_specs=anywhere,
        out_shape=jax.ShapeDtypeStruct((GROUPS, ROWS, LANES), F32),
        scratch_shapes=[
            pltpu.VMEM((GROUPS, ROWS, LANES), F32),
            pltpu.VMEM((GROUPS, ROWS, LANES), F32),
            pltpu.SemaphoreType.DMA((GROUPS,)),
            pltpu.SemaphoreType.DMA((GROUPS,)),
        ],
        cost_estimate=pl.CostEstimate(flops=0, bytes_accessed=1600000, transcendentals=0),
        name="pack",
    )(field)


def trace_kernel(rotor_ref, packed_ref, out_ref, top_ref):
    zeros = jnp.zeros((LANES - ROWS, LANES), F32)
    for block in range(GROUPS):
        turned = jnp.concatenate([packed_ref[block], zeros], 0).T
        top_ref[pl.ds(block * 16, 8), :] = turned[56:64]
        top_ref[pl.ds(block * 16 + 8, 8), :] = turned[120:128]
    for slot in range(32):
        start = pl.multiple_of(rotor_ref[slot] * 8, 8)
        out_ref[pl.ds(slot * 8, 8), :] = top_ref[pl.ds(start, 8), :]


def traces(rotor_element, packed):
    return pl.pallas_call(
        trace_kernel,
        in_specs=[pl.BlockSpec(memory_space=SMEM), pl.BlockSpec(memory_space=VMEM)],
        out_specs=pl.BlockSpec(memory_space=VMEM),
        out_shape=jax.ShapeDtypeStruct((256, LANES), F32),
        scratch_shapes=[pltpu.VMEM((256, LANES), F32)],
        cost_estimate=pl.CostEstimate(flops=0, bytes_accessed=8000000, transcendentals=0),
        name="traces",
    )(rotor_element, packed)


def helm_kernel(
    metric_ref, area_ref, stator_ref, packed_ref, visc_ref, weight_ref, forward_ref, back_ref, out_ref
):
    step = packed_ref.shape[0]
    first = pl.program_id(0) * step
    four = lax.axis_index("four")
    row = lax.broadcasted_iota(jnp.int32, (ROWS, LANES), 0)
    inner = row % 32
    number = jnp.where(
        (inner == 16) & (four == 0), MODES // 2, four * 16 + inner % 16
    )
    wave = number.astype(F32) / KZ_DIV
    wave_sq = wave * wave
    lane = lax.broadcasted_iota(jnp.int32, (1, LANES), 1)
    bottom = lane % 64 < NQ
    field = packed_ref[...].reshape(step * ROWS, LANES)
    grads = dot(left_split(field), forward_ref[...])
    masses, fluxes = [], []
    for block in range(step):
        pair = (first + block) * 2
        rx, ry, sx, sy = [
            lane_scalars(metric_ref[i, pair], metric_ref[i, pair + 1]) for i in range(4)
        ]
        count_a, count_b = jnp.int32(0), jnp.int32(0)
        for edge in range(32):
            here = stator_ref[edge]
            count_a = count_a + jnp.where(here == pair, 1, 0)
            count_b = count_b + jnp.where(here == pair + 1, 1, 0)
        count = lane_scalars(count_a, count_b).astype(F32)
        own = jnp.where(bottom, TAU_COEF * count, 0.0)
        area = lane_scalars(area_ref[pair], area_ref[pair + 1])
        weight = area * weight_ref[...]
        viscous = weight * visc_ref[pl.ds(first + block, 1), :]
        rows = slice(block * ROWS, (block + 1) * ROWS)
        grad_xi, grad_eta = grads[rows, :LANES], grads[rows, LANES:]
        cross = viscous * (rx * sx + ry * sy)
        flux_xi = (viscous * (rx * rx + ry * ry)) * grad_xi + cross * grad_eta
        flux_eta = cross * grad_xi + (viscous * (sx * sx + sy * sy)) * grad_eta
        fluxes.append(jnp.concatenate([flux_xi, flux_eta], 1))
        masses.append((weight * LAMBDA_COEF + own + viscous * wave_sq) * field[rows])
    stiff = dot(left_split(jnp.concatenate(fluxes, 0)), back_ref[...])
    for block in range(step):
        out_ref[block] = masses[block] + stiff[block * ROWS : (block + 1) * ROWS]


def helmholtz(metric, area, stator_element, packed, visc, weight, forward, back):
    step = 4
    return pl.pallas_call(
        helm_kernel,
        grid=(GROUPS // step,),
        in_specs=[
            pl.BlockSpec(memory_space=SMEM),
            pl.BlockSpec(memory_space=SMEM),
            pl.BlockSpec(memory_space=SMEM),
            pl.BlockSpec((step, ROWS, LANES), lambda i: (i, 0, 0)),
            pl.BlockSpec((GROUPS, LANES), lambda i: (0, 0)),
            pl.BlockSpec((1, LANES), lambda i: (0, 0)),
            pl.BlockSpec((3 * LANES, 2 * LANES), lambda i: (0, 0)),
            pl.BlockSpec((6 * LANES, LANES), lambda i: (0, 0)),
        ],
        out_specs=pl.BlockSpec((step, ROWS, LANES), lambda i: (i, 0, 0)),
        out_shape=jax.ShapeDtypeStruct((GROUPS, ROWS, LANES), F32),
        cost_estimate=pl.CostEstimate(flops=2000000000, bytes_accessed=8000000, transcendentals=0),
        name="helm",
    )(metric, area, stator_element, packed, visc, weight, forward, back)


def plane_kernel(
    metric_ref, got_ref, cos_ref, sin_ref, cos_back_ref, sin_back_ref, forward_ref, out_ref
):
    pair = lax.axis_index("four") * 2
    rx, ry, sx, sy = [
        lane_scalars(metric_ref[i, pair], metric_ref[i, pair + 1]) for i in range(4)
    ]
    number = lax.broadcasted_iota(jnp.int32, (PAIRS, LANES), 0)
    wave = number.astype(F32) / KZ_DIV
    sign = jnp.where(number % 2 == 0, 1.0, -1.0).astype(F32)
    plane = lax.broadcasted_iota(jnp.int32, (HALF, LANES), 0)
    third = jnp.where(plane % 3 == 0, 1.0, -0.5).astype(F32)
    is_first = plane == 0
    evens, odds = [], []
    for component in range(3):
        evens.append(got_ref[:, pl.ds(component * 32, 16), :].reshape(PAIRS, LANES))
        odds.append(got_ref[:, pl.ds(component * 32 + 16, 16), :].reshape(PAIRS, LANES))
    evens_z = [wave * odd for odd in odds]
    odds_z = [-wave * even for even in evens]
    last_cos = [odd[0:1] for odd in odds]
    even_all = jnp.concatenate(evens + evens_z, 1)
    odd_all = jnp.concatenate(odds + odds_z, 1)
    cos_part = dot(cos_ref[...], right_split(even_all))
    sin_part = dot(sin_ref[...], right_split(odd_all))
    plus, minus = [], []
    for index in range(6):
        lanes = slice(index * LANES, (index + 1) * LANES)
        cos_here, sin_here = cos_part[:, lanes], sin_part[:, lanes]
        middle = jnp.sum(sign * (evens + evens_z)[index], 0, keepdims=True)
        if index < 3:
            cos_here = cos_here + third * last_cos[index]
            middle = middle + last_cos[index]
        plus.append(cos_here + sin_here)
        minus.append(jnp.where(is_first, middle, cos_here - sin_here))

    def advect(values):
        along_xi = values[0] * rx + values[1] * ry
        along_eta = values[0] * sx + values[1] * sy
        results = []
        for component in range(3):
            grads = dot(left_split(values[component]), forward_ref[...])
            results.append(
                along_xi * grads[:, :LANES]
                + along_eta * grads[:, LANES:]
                + values[2] * values[3 + component]
            )
        return results

    ahead, mirrored = advect(plus), advect(minus)
    middles = [value[0:1] for value in mirrored]
    mirrored = [jnp.where(is_first, 0.0, value) for value in mirrored]
    even_sum = [a + b for a, b in zip(ahead, mirrored)]
    odd_sum = [a - b for a, b in zip(ahead, mirrored)]
    even_out = dot(cos_back_ref[...], right_split(jnp.concatenate(even_sum, 1)))
    odd_out = dot(sin_back_ref[...], right_split(jnp.concatenate(odd_sum, 1)))
    scale = jnp.where(number == 0, 1.0 / PLANES, 2.0 / PLANES).astype(F32)
    for component in range(3):
        lanes = slice(component * LANES, (component + 1) * LANES)
        even_here = even_out[:, lanes] + (scale * sign) * middles[component]
        last = (2.0 / PLANES) * (
            jnp.sum(third * even_sum[component], 0, keepdims=True) + middles[component]
        )
        odd_here = jnp.where(number == 0, last, odd_out[:, lanes])
        out_ref[:, pl.ds(component * 32, 16), :] = even_here.reshape(GROUPS, 16, LANES)
        out_ref[:, pl.ds(component * 32 + 16, 16), :] = odd_here.reshape(GROUPS, 16, LANES)


def planes(metric, got, cosine, sine, cos_back, sin_back, forward):
    whole = pl.BlockSpec(memory_space=VMEM)
    return pl.pallas_call(
        plane_kernel,
        in_specs=[pl.BlockSpec(memory_space=SMEM)] + [whole] * 6,
        out_specs=whole,
        out_shape=jax.ShapeDtypeStruct((GROUPS, ROWS, LANES), F32),
        compiler_params=pltpu.CompilerParams(vmem_limit_bytes=48 * 1024 * 1024),
        cost_estimate=pl.CostEstimate(flops=3000000000, bytes_accessed=4000000, transcendentals=0),
        name="planes",
    )(metric, got, cosine, sine, cos_back, sin_back, forward)


def penalty_kernel(
    source_ref, stator_ref, offset_ref, interp_ref, pieces_ref, helm_ref, out_ref,
    received_ref, base_ref, place_ref,
):
    for edge in range(32):
        rows = pl.ds(edge * 8, 8)
        start = pl.multiple_of(source_ref[edge] * 8, 8)
        received_ref[rows, :] = pieces_ref[pl.ds(start, 8), :]
        base_ref[rows, :] = interp_ref[pl.ds(pl.multiple_of(offset_ref[edge] * 8, 8), 8), :]
        place_ref[rows, :] = jnp.full((8, LANES), stator_ref[edge], jnp.int32)
    lane = lax.broadcasted_iota(jnp.int32, (256, LANES), 1)
    home = place_ref[...] - jnp.where(lane < 64, 0, 1)
    base = base_ref[...]
    left = left_split(received_ref[...].T[:ROWS])
    for block in range(GROUPS):
        matrix = jnp.where(home == 2 * block, base, 0.0)
        high, low = split(matrix)
        right = jnp.concatenate([high, low, high], 0)
        out_ref[block] = helm_ref[block] - dot(left, right)


def penalty(stator_source, stator_element, mortar_offset, interp, pieces, helm):
    whole = pl.BlockSpec(memory_space=VMEM)
    scalars = pl.BlockSpec(memory_space=SMEM)
    return pl.pallas_call(
        penalty_kernel,
        in_specs=[scalars] * 3 + [whole] * 3,
        out_specs=whole,
        out_shape=jax.ShapeDtypeStruct((GROUPS, ROWS, LANES), F32),
        scratch_shapes=[
            pltpu.VMEM((256, LANES), F32),
            pltpu.VMEM((256, LANES), F32),
            pltpu.VMEM((256, LANES), jnp.int32),
        ],
        cost_estimate=pl.CostEstimate(flops=1000000000, bytes_accessed=8000000, transcendentals=0),
        name="penalty",
    )(stator_source, stator_element, mortar_offset, interp, pieces, helm)


def sum_kernel(nonlinear_ref, rest_ref, out_ref, done_ref, out_sems):
    def store(block):
        return pltpu.make_async_copy(
            done_ref.at[block], out_ref.at[:, pl.ds(block * LANES, LANES)], out_sems.at[block]
        )

    for block in range(GROUPS):
        value = -nonlinear_ref[block] - rest_ref[block]
        for component in range(3):
            for parity in range(2):
                start = component * 32 + parity * 16
                done_ref[block, pl.ds(component * 32 + parity, 16, stride=2), :] = value[
                    start : start + 16
                ]
        store(block).start()
    for block in range(GROUPS):
        store(block).wait()


def final_sum(nonlinear, rest):
    whole = pl.BlockSpec(memory_space=VMEM)
    return pl.pallas_call(
        sum_kernel,
        in_specs=[whole, whole],
        out_specs=pl.BlockSpec(memory_space=pl.ANY),
        out_shape=jax.ShapeDtypeStruct((ROWS, GROUPS * LANES), F32),
        scratch_shapes=[
            pltpu.VMEM((GROUPS, ROWS, LANES), F32),
            pltpu.SemaphoreType.DMA((GROUPS,)),
        ],
        cost_estimate=pl.CostEstimate(flops=0, bytes_accessed=2400000, transcendentals=0),
        name="final_sum",
    )(nonlinear, rest)


def local(vel_hat, metric, area, visc, rotor_element, stator_element, mortar_offset, stator_source):
    along_xi, along_eta, node_weight, interp = element_tables()
    cosine, sine, cos_back, sin_back = span_tables()
    forward = as_right(np.concatenate([along_xi.T, along_eta.T], 1))
    back = as_right(np.concatenate([along_xi, along_eta], 0))
    weight = jnp.asarray(np.tile(node_weight, 2)[None, :], F32)
    spread = np.zeros((NQ, NQ, LANES))
    spread[:, :, 0:NQ] = TAU_COEF * interp.transpose(0, 2, 1)
    spread[:, :, 64 : 64 + NQ] = TAU_COEF * interp.transpose(0, 2, 1)
    spread = jnp.asarray(spread.reshape(NQ * NQ, LANES), F32)

    packed = pack(vel_hat.reshape(ROWS, GROUPS * LANES))
    got = lax.all_to_all(packed, "four", 0, 0, tiled=True)
    trace = traces(rotor_element, packed)
    pieces = lax.all_gather(trace, "elem", axis=0, tiled=True)
    helm = helmholtz(
        metric, area, stator_element, packed, visc.reshape(GROUPS, LANES), weight, forward, back
    )
    advect_hat = planes(
        metric, got, as_left(cosine), as_left(sine), as_left(cos_back), as_left(sin_back), forward
    )
    nonlinear = lax.all_to_all(advect_hat, "four", 0, 0, tiled=True)
    rest = penalty(stator_source, stator_element, mortar_offset, spread, pieces, helm)
    return final_sum(nonlinear, rest).reshape(vel_hat.shape)


def solution(mesh):
    in_specs = (
        P(None, "four", "elem"),
        P(None, "elem"),
        P("elem"),
        P("elem"),
        P("elem"),
        P("elem"),
        P("elem"),
        P("elem"),
    )
    out_specs = P(None, "four", "elem")
    return jax.shard_map(local, mesh=mesh, in_specs=in_specs, out_specs=out_specs, check_vma=False)
```

```python
import math

import jax
import jax.numpy as jnp
import numpy as np
from jax import lax
from jax.experimental import pallas as pl
from jax.experimental.pallas import tpu as pltpu
from jax.sharding import PartitionSpec as P

NQ = 8
MODES = 512
PLANES = 768
HALF = PLANES // 2
PAIRS = MODES // 2
HELD = 9
RING = 8
GROUPS = 16
ROWS = 96
LANES = 128

LAMBDA_COEF = 10.0
TAU_COEF = 2.0
KZ_DIV = 32.0

F32 = jnp.float32
BF16 = jnp.bfloat16
VMEM = pltpu.MemorySpace.VMEM
SMEM = pltpu.MemorySpace.SMEM


def element_tables():
    order = NQ - 1
    points = -np.cos(np.pi * np.arange(NQ) / order)
    barycentric = np.array([(-1.0) ** index_a for index_a in range(NQ)])
    barycentric[0] *= 0.5
    barycentric[-1] *= 0.5
    derivative = np.zeros((NQ, NQ))
    for index_a in range(NQ):
        for index_b in range(NQ):
            if index_a != index_b:
                derivative[index_a, index_b] = (
                    barycentric[index_b]
                    / barycentric[index_a]
                    / (points[index_a] - points[index_b])
                )
        derivative[index_a, index_a] = -np.sum(derivative[index_a])
    angles = np.pi * np.arange(NQ) / order
    weights = np.ones(NQ)
    for harmonic in range(1, order // 2 + 1):
        weights = weights - 2.0 * np.cos(2 * harmonic * angles) / (4 * harmonic * harmonic - 1)
    weights = weights * 2.0 / order
    weights[0] *= 0.5
    weights[-1] *= 0.5
    identity = np.eye(NQ)
    along_xi = np.kron(np.eye(2), np.kron(identity, derivative))
    along_eta = np.kron(np.eye(2), np.kron(derivative, identity))
    node_weight = np.kron(weights, weights)
    interp = np.ones((NQ, NQ, NQ))
    for offset in range(NQ):
        targets = points * (1.0 - offset / 16.0) + offset / 16.0
        for index_a in range(NQ):
            for index_b in range(NQ):
                for index_c in range(NQ):
                    if index_c != index_b:
                        interp[offset, index_a, index_b] *= (targets[index_a] - points[index_c]) / (
                            points[index_b] - points[index_c]
                        )
    return along_xi, along_eta, node_weight, interp


def two_parts(table):
    table = np.asarray(table, np.float32)
    high = table.astype(BF16)
    low = (table - high.astype(np.float32)).astype(BF16)
    return high, low


def as_left(table):
    high, low = two_parts(table)
    return jnp.asarray(np.concatenate([high, low, high], 1))


def as_right(table):
    high, low = two_parts(table)
    return jnp.asarray(np.concatenate([high, low, high], 0))


def span_tables():
    plane = np.arange(HALF)[:, None]
    number = np.arange(PAIRS)[None, :]
    angle = 2.0 * np.pi * ((plane * number) % PLANES) / PLANES
    cosine, sine = np.cos(angle), np.sin(angle)
    scale = np.full((PAIRS, 1), 2.0 / PLANES)
    scale[0] = 1.0 / PLANES
    return cosine, sine, cosine.T * scale, sine.T * (2.0 / PLANES)


def split(value):
    high = value.astype(BF16)
    low = (value - high.astype(F32)).astype(BF16)
    return high, low


def dot(left, right):
    return jnp.dot(left, right, preferred_element_type=F32)


def left_split(value):
    high, low = split(value)
    return jnp.concatenate([high, high, low], -1)


def right_split(value):
    high, low = split(value)
    return jnp.concatenate([high, high, low], 0)


def lane_scalars(first, second):
    lane = lax.broadcasted_iota(jnp.int32, (1, LANES), 1)
    return jnp.where(lane < LANES // 2, first, second)


def pack_kernel(field_ref, out_ref, held_ref, in_sems, out_sems):
    loads = [
        pltpu.make_async_copy(
            field_ref.at[:, pl.ds(block * LANES, LANES)], held_ref.at[block], in_sems.at[block]
        )
        for block in range(GROUPS)
    ]
    stores = [
        pltpu.make_async_copy(held_ref.at[block], out_ref.at[block], out_sems.at[block])
        for block in range(GROUPS)
    ]
    for load in loads:
        load.start()
    for load, store in zip(loads, stores):
        load.wait()
        store.start()
    for store in stores:
        store.wait()


def pack(field):
    anywhere = pl.BlockSpec(memory_space=pl.ANY)
    return pl.pallas_call(
        pack_kernel,
        in_specs=[anywhere],
        out_specs=anywhere,
        out_shape=jax.ShapeDtypeStruct((GROUPS, ROWS, LANES), F32),
        scratch_shapes=[
            pltpu.VMEM((GROUPS, ROWS, LANES), F32),
            pltpu.SemaphoreType.DMA((GROUPS,)),
            pltpu.SemaphoreType.DMA((GROUPS,)),
        ],
        cost_estimate=pl.CostEstimate(flops=0, bytes_accessed=1600000, transcendentals=0),
        name="pack",
    )(field)


def trace_kernel(rotor_ref, packed_ref, out_ref, top_ref):
    lane = lax.broadcasted_iota(jnp.int32, (ROWS, LANES), 1)
    zeros = jnp.zeros((LANES - ROWS, LANES), F32)
    for half in range(2):
        rows = jnp.zeros((ROWS, LANES), F32)
        for block in range(8):
            field = packed_ref[half * 8 + block]
            low = pltpu.roll(field, (16 * block - 56) % LANES, 1)
            high = pltpu.roll(field, (16 * block + 8 - 120) % LANES, 1)
            rows = jnp.where(lane // 8 == 2 * block, low, rows)
            rows = jnp.where(lane // 8 == 2 * block + 1, high, rows)
        top_ref[pl.ds(half * LANES, LANES), :] = jnp.concatenate([rows, zeros], 0).T
    for slot in range(32):
        start = pl.multiple_of(rotor_ref[slot] * 8, 8)
        out_ref[pl.ds(slot * 8, 8), :] = top_ref[pl.ds(start, 8), :]


def traces(rotor_element, packed):
    return pl.pallas_call(
        trace_kernel,
        in_specs=[pl.BlockSpec(memory_space=SMEM), pl.BlockSpec(memory_space=VMEM)],
        out_specs=pl.BlockSpec(memory_space=VMEM),
        out_shape=jax.ShapeDtypeStruct((256, LANES), F32),
        scratch_shapes=[pltpu.VMEM((256, LANES), F32)],
        cost_estimate=pl.CostEstimate(flops=0, bytes_accessed=8000000, transcendentals=0),
        name="traces",
    )(rotor_element, packed)


def pair_kernel(mine_ref, other_ref, out_ref):
    out_ref[pl.ds(0, 256), :] = mine_ref[...]
    out_ref[pl.ds(256, 256), :] = other_ref[...]


def pair(mine, other):
    whole = pl.BlockSpec(memory_space=VMEM)
    return pl.pallas_call(
        pair_kernel,
        in_specs=[whole, whole],
        out_specs=whole,
        out_shape=jax.ShapeDtypeStruct((512, LANES), F32),
        cost_estimate=pl.CostEstimate(flops=0, bytes_accessed=1000000, transcendentals=0),
        name="pair",
    )(mine, other)


def moves(distance, cores=(0, 1)):
    return [
        (2 * z + c, 2 * ((z + (distance if c == 0 else -distance)) % RING) + c)
        for z in range(RING)
        for c in cores
    ]


ACROSS = [(i, i ^ 1) for i in range(2 * RING)]


def helm_kernel(
    metric_ref, area_ref, stator_ref, packed_ref, visc_ref, weight_ref, forward_ref, back_ref, out_ref,
    count_ref,
):
    step = packed_ref.shape[0]
    first = pl.program_id(0) * step

    @pl.when(pl.program_id(0) == 0)
    def _():
        for element in range(32):
            count_ref[element] = 0
        for edge in range(32):
            count_ref[stator_ref[edge]] = count_ref[stator_ref[edge]] + 1

    four = lax.axis_index("four")
    row = lax.broadcasted_iota(jnp.int32, (ROWS, LANES), 0)
    inner = row % 32
    number = jnp.where((inner == 1) & (four == 0), MODES // 2, four * 16 + inner // 2)
    wave = number.astype(F32) / KZ_DIV
    wave_sq = wave * wave
    lane = lax.broadcasted_iota(jnp.int32, (1, LANES), 1)
    bottom = lane % 64 < NQ
    field = packed_ref[...].reshape(step * ROWS, LANES)
    grads = dot(left_split(field), forward_ref[...])
    masses, fluxes = [], []
    for block in range(step):
        pair = (first + block) * 2
        rx, ry, sx, sy = [
            lane_scalars(metric_ref[i, pair], metric_ref[i, pair + 1]) for i in range(4)
        ]
        count = lane_scalars(count_ref[pair], count_ref[pair + 1]).astype(F32)
        own = jnp.where(bottom, TAU_COEF * count, 0.0)
        area = lane_scalars(area_ref[pair], area_ref[pair + 1])
        weight = area * weight_ref[...]
        viscous = weight * visc_ref[pl.ds(first + block, 1), :]
        rows = slice(block * ROWS, (block + 1) * ROWS)
        grad_xi, grad_eta = grads[rows, :LANES], grads[rows, LANES:]
        cross = viscous * (rx * sx + ry * sy)
        flux_xi = (viscous * (rx * rx + ry * ry)) * grad_xi + cross * grad_eta
        flux_eta = cross * grad_xi + (viscous * (sx * sx + sy * sy)) * grad_eta
        fluxes.append(jnp.concatenate([flux_xi, flux_eta], 1))
        masses.append((weight * LAMBDA_COEF + own + viscous * wave_sq) * field[rows])
    stiff = dot(left_split(jnp.concatenate(fluxes, 0)), back_ref[...])
    for block in range(step):
        out_ref[block] = masses[block] + stiff[block * ROWS : (block + 1) * ROWS]


def helmholtz(metric, area, stator_element, packed, visc, weight, forward, back):
    step = 4
    return pl.pallas_call(
        helm_kernel,
        grid=(GROUPS // step,),
        in_specs=[
            pl.BlockSpec(memory_space=SMEM),
            pl.BlockSpec(memory_space=SMEM),
            pl.BlockSpec(memory_space=SMEM),
            pl.BlockSpec((step, ROWS, LANES), lambda i: (i, 0, 0)),
            pl.BlockSpec((GROUPS, LANES), lambda i: (0, 0)),
            pl.BlockSpec((1, LANES), lambda i: (0, 0)),
            pl.BlockSpec((3 * LANES, 2 * LANES), lambda i: (0, 0)),
            pl.BlockSpec((6 * LANES, LANES), lambda i: (0, 0)),
        ],
        out_specs=pl.BlockSpec((step, ROWS, LANES), lambda i: (i, 0, 0)),
        out_shape=jax.ShapeDtypeStruct((GROUPS, ROWS, LANES), F32),
        scratch_shapes=[pltpu.SMEM((32,), jnp.int32)],
        cost_estimate=pl.CostEstimate(flops=2000000000, bytes_accessed=8000000, transcendentals=0),
        name="helm",
    )(metric, area, stator_element, packed, visc, weight, forward, back)


def plane_kernel(
    metric_ref, got_ref, cos_ref, sin_ref, cos_back_ref, sin_back_ref, forward_ref, out_ref
):
    pair = lax.axis_index("four") * 2
    rx, ry, sx, sy = [
        lane_scalars(metric_ref[i, pair], metric_ref[i, pair + 1]) for i in range(4)
    ]
    number = lax.broadcasted_iota(jnp.int32, (PAIRS, LANES), 0)
    wave = number.astype(F32) / KZ_DIV
    sign = jnp.where(number % 2 == 0, 1.0, -1.0).astype(F32)
    plane = lax.broadcasted_iota(jnp.int32, (HALF, LANES), 0)
    third = jnp.where(plane % 3 == 0, 1.0, -0.5).astype(F32)
    is_first = plane == 0
    evens, odds = [], []
    for component in range(3):
        start = component * 32
        evens.append(got_ref[:, pl.ds(start, 16, stride=2), :].reshape(PAIRS, LANES))
        odds.append(got_ref[:, pl.ds(start + 1, 16, stride=2), :].reshape(PAIRS, LANES))
    evens_z = [wave * odd for odd in odds]
    odds_z = [-wave * even for even in evens]
    last_cos = [odd[0:1] for odd in odds]
    even_all = jnp.concatenate(evens + evens_z, 1)
    odd_all = jnp.concatenate(odds + odds_z, 1)
    cos_part = dot(cos_ref[...], right_split(even_all))
    sin_part = dot(sin_ref[...], right_split(odd_all))
    plus, minus = [], []
    for index in range(6):
        lanes = slice(index * LANES, (index + 1) * LANES)
        cos_here, sin_here = cos_part[:, lanes], sin_part[:, lanes]
        middle = jnp.sum(sign * (evens + evens_z)[index], 0, keepdims=True)
        if index < 3:
            cos_here = cos_here + third * last_cos[index]
            middle = middle + last_cos[index]
        plus.append(cos_here + sin_here)
        minus.append(jnp.where(is_first, middle, cos_here - sin_here))

    def advect(values):
        along_xi = values[0] * rx + values[1] * ry
        along_eta = values[0] * sx + values[1] * sy
        results = []
        for component in range(3):
            grads = dot(left_split(values[component]), forward_ref[...])
            results.append(
                along_xi * grads[:, :LANES]
                + along_eta * grads[:, LANES:]
                + values[2] * values[3 + component]
            )
        return results

    ahead, mirrored = advect(plus), advect(minus)
    middles = [value[0:1] for value in mirrored]
    mirrored = [jnp.where(is_first, 0.0, value) for value in mirrored]
    even_sum = [a + b for a, b in zip(ahead, mirrored)]
    odd_sum = [a - b for a, b in zip(ahead, mirrored)]
    even_out = dot(cos_back_ref[...], right_split(jnp.concatenate(even_sum, 1)))
    odd_out = dot(sin_back_ref[...], right_split(jnp.concatenate(odd_sum, 1)))
    scale = jnp.where(number == 0, 1.0 / PLANES, 2.0 / PLANES).astype(F32)
    for component in range(3):
        lanes = slice(component * LANES, (component + 1) * LANES)
        even_here = even_out[:, lanes] + (scale * sign) * middles[component]
        last = (2.0 / PLANES) * (
            jnp.sum(third * even_sum[component], 0, keepdims=True) + middles[component]
        )
        odd_here = jnp.where(number == 0, last, odd_out[:, lanes])
        start = component * 32
        out_ref[:, pl.ds(start, 16, stride=2), :] = even_here.reshape(GROUPS, 16, LANES)
        out_ref[:, pl.ds(start + 1, 16, stride=2), :] = odd_here.reshape(GROUPS, 16, LANES)


def planes(metric, got, cosine, sine, cos_back, sin_back, forward):
    whole = pl.BlockSpec(memory_space=VMEM)
    return pl.pallas_call(
        plane_kernel,
        in_specs=[pl.BlockSpec(memory_space=SMEM)] + [whole] * 6,
        out_specs=whole,
        out_shape=jax.ShapeDtypeStruct((GROUPS, ROWS, LANES), F32),
        compiler_params=pltpu.CompilerParams(vmem_limit_bytes=48 * 1024 * 1024),
        cost_estimate=pl.CostEstimate(flops=3000000000, bytes_accessed=4000000, transcendentals=0),
        name="planes",
    )(metric, got, cosine, sine, cos_back, sin_back, forward)


def penalty_kernel(source_ref, stator_ref, offset_ref, interp_ref, *refs):
    piece_refs, refs = refs[:HELD], refs[HELD:]
    helm_ref, out_ref, received_ref, base_ref, place_ref = refs
    elem = lax.axis_index("elem")
    for edge in range(32):
        rows = pl.ds(edge * 8, 8)
        base_ref[rows, :] = interp_ref[pl.ds(pl.multiple_of(offset_ref[edge] * 8, 8), 8), :]
        place_ref[rows, :] = jnp.full((8, 256), stator_ref[edge], jnp.int32)
    lane = lax.broadcasted_iota(jnp.int32, (256, 256), 1)
    matrix = jnp.where(place_ref[...] == lane // 8, base_ref[...], 0.0)
    high, low = split(matrix)
    right = jnp.concatenate([high, low, high], 0)
    core = elem % 2
    for edge in range(32):
        source = source_ref[edge]
        owner, slot = source // 32, source % 32
        owner_core = owner % 2
        behind = (elem // 2 - owner // 2 + RING) % RING
        near = jnp.where(behind <= 4, behind, RING - behind)
        side = jnp.where(
            behind == 0, core, jnp.where(behind == 4, owner_core, jnp.where(behind < 4, 0, 1))
        )
        piece = jnp.where((behind == 0) | (side == core), near, near + 4)
        first = pl.multiple_of(slot * 8, 8)
        start = pl.multiple_of((jnp.where(side == owner_core, 0, 32) + slot) * 8, 8)
        tile = piece_refs[0][pl.ds(start, 8), :]
        for index in range(1, HELD):
            at = first if index % 4 == 0 else start
            tile = jnp.where(piece == index, piece_refs[index][pl.ds(at, 8), :], tile)
        received_ref[pl.ds(edge * 8, 8), :] = tile
    placed = dot(left_split(received_ref[...].T[:ROWS]), right)
    lane = lax.broadcasted_iota(jnp.int32, (ROWS, LANES), 1)
    for block in range(GROUPS):
        half = placed[:, (block // 8) * LANES : (block // 8 + 1) * LANES]
        start = 16 * (block % 8)
        low = pltpu.roll(half, (-start) % LANES, 1)
        high = pltpu.roll(half, (64 - 8 - start) % LANES, 1)
        value = jnp.where(lane < 8, low, jnp.where(lane // 8 == 8, high, 0.0))
        out_ref[block] = helm_ref[block] - value


def penalty(stator_source, stator_element, mortar_offset, interp, pieces, helm):
    whole = pl.BlockSpec(memory_space=VMEM)
    scalars = pl.BlockSpec(memory_space=SMEM)
    return pl.pallas_call(
        penalty_kernel,
        in_specs=[scalars] * 3 + [whole] * (HELD + 2),
        out_specs=whole,
        out_shape=jax.ShapeDtypeStruct((GROUPS, ROWS, LANES), F32),
        scratch_shapes=[
            pltpu.VMEM((256, LANES), F32),
            pltpu.VMEM((256, 256), F32),
            pltpu.VMEM((256, 256), jnp.int32),
        ],
        cost_estimate=pl.CostEstimate(flops=1000, bytes_accessed=1000, transcendentals=0),
        name="penalty",
    )(stator_source, stator_element, mortar_offset, interp, *pieces, helm)


def sum_kernel(nonlinear_ref, rest_ref, out_ref, in_ref, done_ref, in_sems, out_sems):
    loads = [
        pltpu.make_async_copy(nonlinear_ref.at[block], in_ref.at[block], in_sems.at[block])
        for block in range(GROUPS)
    ]
    stores = [
        pltpu.make_async_copy(
            done_ref.at[block], out_ref.at[:, pl.ds(block * LANES, LANES)], out_sems.at[block]
        )
        for block in range(GROUPS)
    ]
    for load in loads:
        load.start()
    for block in range(GROUPS):
        loads[block].wait()
        done_ref[block] = -in_ref[block] - rest_ref[block]
        stores[block].start()
    for store in stores:
        store.wait()


def final_sum(nonlinear, rest):
    anywhere = pl.BlockSpec(memory_space=pl.ANY)
    return pl.pallas_call(
        sum_kernel,
        in_specs=[anywhere, pl.BlockSpec(memory_space=VMEM)],
        out_specs=anywhere,
        out_shape=jax.ShapeDtypeStruct((ROWS, GROUPS * LANES), F32),
        scratch_shapes=[
            pltpu.VMEM((GROUPS, ROWS, LANES), F32),
            pltpu.VMEM((GROUPS, ROWS, LANES), F32),
            pltpu.SemaphoreType.DMA((GROUPS,)),
            pltpu.SemaphoreType.DMA((GROUPS,)),
        ],
        cost_estimate=pl.CostEstimate(flops=0, bytes_accessed=2400000, transcendentals=0),
        name="final_sum",
    )(nonlinear, rest)


def local(vel_hat, metric, area, visc, rotor_element, stator_element, mortar_offset, stator_source):
    along_xi, along_eta, node_weight, interp = element_tables()
    cosine, sine, cos_back, sin_back = span_tables()
    forward = as_right(np.concatenate([along_xi.T, along_eta.T], 1))
    back = as_right(np.concatenate([along_xi, along_eta], 0))
    weight = jnp.asarray(np.tile(node_weight, 2)[None, :], F32)
    spread = np.tile(TAU_COEF * interp.transpose(0, 2, 1), (1, 1, 32))
    spread = jnp.asarray(spread.reshape(NQ * NQ, 256), F32)

    packed = pack(vel_hat.reshape(ROWS, GROUPS * LANES))
    got = lax.all_to_all(packed, "four", 0, 0, tiled=True)
    mine = traces(rotor_element, packed)
    both = pair(mine, lax.ppermute(mine, "elem", ACROSS))
    one = lax.ppermute(both, "elem", moves(1))
    two = lax.ppermute(both, "elem", moves(2))
    helm = helmholtz(
        metric, area, stator_element, packed, visc.reshape(GROUPS, LANES), weight, forward, back
    )
    got, helm = lax.optimization_barrier((got, helm))
    advect_hat = planes(
        metric, got, as_left(cosine), as_left(sine), as_left(cos_back), as_left(sin_back), forward
    )
    nonlinear = lax.all_to_all(advect_hat, "four", 0, 0, tiled=True)
    three = lax.ppermute(two, "elem", moves(1))
    four = lax.ppermute(two[:256], "elem", moves(2))
    held = [one, two, three, four]
    pieces = [both] + held + [lax.ppermute(piece, "elem", ACROSS) for piece in held]
    rest = penalty(stator_source, stator_element, mortar_offset, spread, pieces, helm)
    return final_sum(nonlinear, rest).reshape(vel_hat.shape)


def solution(mesh):
    in_specs = (
        P(None, "four", "elem"),
        P(None, "elem"),
        P("elem"),
        P("elem"),
        P("elem"),
        P("elem"),
        P("elem"),
        P("elem"),
    )
    out_specs = P(None, "four", "elem")
    return jax.shard_map(local, mesh=mesh, in_specs=in_specs, out_specs=out_specs, check_vma=False)
```

```python
import math

import jax
import jax.numpy as jnp
import numpy as np
from jax import lax
from jax.experimental import pallas as pl
from jax.experimental.pallas import tpu as pltpu
from jax.sharding import PartitionSpec as P

NQ = 8
MODES = 512
PLANES = 768
HALF = PLANES // 2
PAIRS = MODES // 2
HELD = 9
RING = 8
GROUPS = 16
ROWS = 96
LANES = 128

LAMBDA_COEF = 10.0
TAU_COEF = 2.0
KZ_DIV = 32.0

F32 = jnp.float32
BF16 = jnp.bfloat16
VMEM = pltpu.MemorySpace.VMEM
SMEM = pltpu.MemorySpace.SMEM


def element_tables():
    order = NQ - 1
    points = -np.cos(np.pi * np.arange(NQ) / order)
    barycentric = np.array([(-1.0) ** index_a for index_a in range(NQ)])
    barycentric[0] *= 0.5
    barycentric[-1] *= 0.5
    derivative = np.zeros((NQ, NQ))
    for index_a in range(NQ):
        for index_b in range(NQ):
            if index_a != index_b:
                derivative[index_a, index_b] = (
                    barycentric[index_b]
                    / barycentric[index_a]
                    / (points[index_a] - points[index_b])
                )
        derivative[index_a, index_a] = -np.sum(derivative[index_a])
    angles = np.pi * np.arange(NQ) / order
    weights = np.ones(NQ)
    for harmonic in range(1, order // 2 + 1):
        weights = weights - 2.0 * np.cos(2 * harmonic * angles) / (4 * harmonic * harmonic - 1)
    weights = weights * 2.0 / order
    weights[0] *= 0.5
    weights[-1] *= 0.5
    identity = np.eye(NQ)
    along_xi = np.kron(np.eye(2), np.kron(identity, derivative))
    along_eta = np.kron(np.eye(2), np.kron(derivative, identity))
    node_weight = np.kron(weights, weights)
    interp = np.ones((NQ, NQ, NQ))
    for offset in range(NQ):
        targets = points * (1.0 - offset / 16.0) + offset / 16.0
        for index_a in range(NQ):
            for index_b in range(NQ):
                for index_c in range(NQ):
                    if index_c != index_b:
                        interp[offset, index_a, index_b] *= (targets[index_a] - points[index_c]) / (
                            points[index_b] - points[index_c]
                        )
    return along_xi, along_eta, node_weight, interp


def two_parts(table):
    table = np.asarray(table, np.float32)
    high = table.astype(BF16)
    low = (table - high.astype(np.float32)).astype(BF16)
    return high, low


def as_left(table):
    high, low = two_parts(table)
    return jnp.asarray(np.concatenate([high, low, high], 1))


def as_right(table):
    high, low = two_parts(table)
    return jnp.asarray(np.concatenate([high, low, high], 0))


def span_tables():
    plane = np.arange(HALF)[:, None]
    number = np.arange(PAIRS)[None, :]
    angle = 2.0 * np.pi * ((plane * number) % PLANES) / PLANES
    cosine, sine = np.cos(angle), np.sin(angle)
    scale = np.full((PAIRS, 1), 2.0 / PLANES)
    scale[0] = 1.0 / PLANES
    return cosine, sine, cosine.T * scale, sine.T * (2.0 / PLANES)


def granted(mebibytes):
    return pltpu.CompilerParams(vmem_limit_bytes=mebibytes * 1024 * 1024)


def split(value):
    high = value.astype(BF16)
    low = (value - high.astype(F32)).astype(BF16)
    return high, low


def dot(left, right):
    return jnp.dot(left, right, preferred_element_type=F32)


def left_split(value):
    high, low = split(value)
    return jnp.concatenate([high, high, low], -1)


def right_split(value):
    high, low = split(value)
    return jnp.concatenate([high, high, low], 0)


def lane_scalars(first, second):
    lane = lax.broadcasted_iota(jnp.int32, (1, LANES), 1)
    return jnp.where(lane < LANES // 2, first, second)


def pack_kernel(field_ref, out_ref, sems):
    loads = [
        pltpu.make_async_copy(
            field_ref.at[:, pl.ds(block * LANES, LANES)], out_ref.at[block], sems.at[block]
        )
        for block in range(GROUPS)
    ]
    for load in loads:
        load.start()
    for load in loads:
        load.wait()


def pack(field):
    return pl.pallas_call(
        pack_kernel,
        in_specs=[pl.BlockSpec(memory_space=pl.ANY)],
        out_specs=pl.BlockSpec(memory_space=VMEM),
        out_shape=jax.ShapeDtypeStruct((GROUPS, ROWS, LANES), F32),
        scratch_shapes=[pltpu.SemaphoreType.DMA((GROUPS,))],
        compiler_params=granted(4),
        cost_estimate=pl.CostEstimate(flops=0, bytes_accessed=1600000, transcendentals=0),
        name="pack",
    )(field)


def trace_kernel(rotor_ref, packed_ref, out_ref, top_ref):
    lane = lax.broadcasted_iota(jnp.int32, (ROWS, LANES), 1)
    zeros = jnp.zeros((LANES - ROWS, LANES), F32)
    for half in range(2):
        rows = jnp.zeros((ROWS, LANES), F32)
        for block in range(8):
            field = packed_ref[half * 8 + block]
            low = pltpu.roll(field, (16 * block - 56) % LANES, 1)
            high = pltpu.roll(field, (16 * block + 8 - 120) % LANES, 1)
            rows = jnp.where(lane // 8 == 2 * block, low, rows)
            rows = jnp.where(lane // 8 == 2 * block + 1, high, rows)
        top_ref[pl.ds(half * LANES, LANES), :] = jnp.concatenate([rows, zeros], 0).T
    for slot in range(32):
        start = pl.multiple_of(rotor_ref[slot] * 8, 8)
        out_ref[pl.ds(slot * 8, 8), :] = top_ref[pl.ds(start, 8), :]


def traces(rotor_element, packed):
    return pl.pallas_call(
        trace_kernel,
        in_specs=[pl.BlockSpec(memory_space=SMEM), pl.BlockSpec(memory_space=VMEM)],
        out_specs=pl.BlockSpec(memory_space=VMEM),
        out_shape=jax.ShapeDtypeStruct((256, LANES), F32),
        scratch_shapes=[pltpu.VMEM((256, LANES), F32)],
        compiler_params=granted(4),
        cost_estimate=pl.CostEstimate(flops=0, bytes_accessed=8000000, transcendentals=0),
        name="traces",
    )(rotor_element, packed)


def pair_kernel(mine_ref, other_ref, out_ref):
    out_ref[pl.ds(0, 256), :] = mine_ref[...]
    out_ref[pl.ds(256, 256), :] = other_ref[...]


def pair(mine, other):
    whole = pl.BlockSpec(memory_space=VMEM)
    return pl.pallas_call(
        pair_kernel,
        in_specs=[whole, whole],
        out_specs=whole,
        out_shape=jax.ShapeDtypeStruct((512, LANES), F32),
        compiler_params=granted(2),
        cost_estimate=pl.CostEstimate(flops=0, bytes_accessed=1000000, transcendentals=0),
        name="pair",
    )(mine, other)


def moves(distance, cores=(0, 1)):
    return [
        (2 * z + c, 2 * ((z + (distance if c == 0 else -distance)) % RING) + c)
        for z in range(RING)
        for c in cores
    ]


ACROSS = [(i, i ^ 1) for i in range(2 * RING)]


def helm_kernel(
    metric_ref, area_ref, stator_ref, packed_ref, visc_ref, weight_ref, forward_ref, back_ref, out_ref,
    count_ref,
):
    step = packed_ref.shape[0]
    first = pl.program_id(0) * step

    @pl.when(pl.program_id(0) == 0)
    def _():
        for element in range(32):
            count_ref[element] = 0
        for edge in range(32):
            count_ref[stator_ref[edge]] = count_ref[stator_ref[edge]] + 1

    four = lax.axis_index("four")
    row = lax.broadcasted_iota(jnp.int32, (ROWS, LANES), 0)
    inner = row % 32
    number = jnp.where((inner == 1) & (four == 0), MODES // 2, four * 16 + inner // 2)
    wave = number.astype(F32) / KZ_DIV
    wave_sq = wave * wave
    lane = lax.broadcasted_iota(jnp.int32, (1, LANES), 1)
    bottom = lane % 64 < NQ
    field = packed_ref[...].reshape(step * ROWS, LANES)
    grads = dot(left_split(field), forward_ref[...])
    masses, fluxes = [], []
    for block in range(step):
        pair = (first + block) * 2
        rx, ry, sx, sy = [
            lane_scalars(metric_ref[i, pair], metric_ref[i, pair + 1]) for i in range(4)
        ]
        count = lane_scalars(count_ref[pair], count_ref[pair + 1]).astype(F32)
        own = jnp.where(bottom, TAU_COEF * count, 0.0)
        area = lane_scalars(area_ref[pair], area_ref[pair + 1])
        weight = area * weight_ref[...]
        viscous = weight * visc_ref[pl.ds(first + block, 1), :]
        rows = slice(block * ROWS, (block + 1) * ROWS)
        grad_xi, grad_eta = grads[rows, :LANES], grads[rows, LANES:]
        cross = viscous * (rx * sx + ry * sy)
        flux_xi = (viscous * (rx * rx + ry * ry)) * grad_xi + cross * grad_eta
        flux_eta = cross * grad_xi + (viscous * (sx * sx + sy * sy)) * grad_eta
        fluxes.append(jnp.concatenate([flux_xi, flux_eta], 1))
        masses.append((weight * LAMBDA_COEF + own + viscous * wave_sq) * field[rows])
    stiff = dot(left_split(jnp.concatenate(fluxes, 0)), back_ref[...])
    for block in range(step):
        out_ref[block] = masses[block] + stiff[block * ROWS : (block + 1) * ROWS]


def helmholtz(metric, area, stator_element, packed, visc, weight, forward, back):
    step = 4
    return pl.pallas_call(
        helm_kernel,
        grid=(GROUPS // step,),
        in_specs=[
            pl.BlockSpec(memory_space=SMEM),
            pl.BlockSpec(memory_space=SMEM),
            pl.BlockSpec(memory_space=SMEM),
            pl.BlockSpec((step, ROWS, LANES), lambda i: (i, 0, 0)),
            pl.BlockSpec((GROUPS, LANES), lambda i: (0, 0)),
            pl.BlockSpec((1, LANES), lambda i: (0, 0)),
            pl.BlockSpec((3 * LANES, 2 * LANES), lambda i: (0, 0)),
            pl.BlockSpec((6 * LANES, LANES), lambda i: (0, 0)),
        ],
        out_specs=pl.BlockSpec((step, ROWS, LANES), lambda i: (i, 0, 0)),
        out_shape=jax.ShapeDtypeStruct((GROUPS, ROWS, LANES), F32),
        scratch_shapes=[pltpu.SMEM((32,), jnp.int32)],
        compiler_params=granted(8),
        cost_estimate=pl.CostEstimate(flops=2000000000, bytes_accessed=8000000, transcendentals=0),
        name="helm",
    )(metric, area, stator_element, packed, visc, weight, forward, back)


def plane_kernel(
    metric_ref, got_ref, cos_ref, sin_ref, cos_back_ref, sin_back_ref, forward_ref, out_ref
):
    pair = lax.axis_index("four") * 2
    rx, ry, sx, sy = [
        lane_scalars(metric_ref[i, pair], metric_ref[i, pair + 1]) for i in range(4)
    ]
    number = lax.broadcasted_iota(jnp.int32, (PAIRS, LANES), 0)
    wave = number.astype(F32) / KZ_DIV
    sign = jnp.where(number % 2 == 0, 1.0, -1.0).astype(F32)
    plane = lax.broadcasted_iota(jnp.int32, (HALF, LANES), 0)
    third = jnp.where(plane % 3 == 0, 1.0, -0.5).astype(F32)
    is_first = plane == 0
    evens, odds = [], []
    for component in range(3):
        start = component * 32
        evens.append(got_ref[:, pl.ds(start, 16, stride=2), :].reshape(PAIRS, LANES))
        odds.append(got_ref[:, pl.ds(start + 1, 16, stride=2), :].reshape(PAIRS, LANES))
    evens_z = [wave * odd for odd in odds]
    odds_z = [-wave * even for even in evens]
    last_cos = [odd[0:1] for odd in odds]
    even_all = jnp.concatenate(evens + evens_z, 1)
    odd_all = jnp.concatenate(odds + odds_z, 1)
    cos_part = dot(cos_ref[...], right_split(even_all))
    sin_part = dot(sin_ref[...], right_split(odd_all))
    plus, minus = [], []
    for index in range(6):
        lanes = slice(index * LANES, (index + 1) * LANES)
        cos_here, sin_here = cos_part[:, lanes], sin_part[:, lanes]
        middle = jnp.sum(sign * (evens + evens_z)[index], 0, keepdims=True)
        if index < 3:
            cos_here = cos_here + third * last_cos[index]
            middle = middle + last_cos[index]
        plus.append(cos_here + sin_here)
        minus.append(jnp.where(is_first, middle, cos_here - sin_here))

    def advect(values):
        along_xi = values[0] * rx + values[1] * ry
        along_eta = values[0] * sx + values[1] * sy
        results = []
        for component in range(3):
            grads = dot(left_split(values[component]), forward_ref[...])
            results.append(
                along_xi * grads[:, :LANES]
                + along_eta * grads[:, LANES:]
                + values[2] * values[3 + component]
            )
        return results

    ahead, mirrored = advect(plus), advect(minus)
    middles = [value[0:1] for value in mirrored]
    mirrored = [jnp.where(is_first, 0.0, value) for value in mirrored]
    even_sum = [a + b for a, b in zip(ahead, mirrored)]
    odd_sum = [a - b for a, b in zip(ahead, mirrored)]
    even_out = dot(cos_back_ref[...], right_split(jnp.concatenate(even_sum, 1)))
    odd_out = dot(sin_back_ref[...], right_split(jnp.concatenate(odd_sum, 1)))
    scale = jnp.where(number == 0, 1.0 / PLANES, 2.0 / PLANES).astype(F32)
    for component in range(3):
        lanes = slice(component * LANES, (component + 1) * LANES)
        even_here = even_out[:, lanes] + (scale * sign) * middles[component]
        last = (2.0 / PLANES) * (
            jnp.sum(third * even_sum[component], 0, keepdims=True) + middles[component]
        )
        odd_here = jnp.where(number == 0, last, odd_out[:, lanes])
        start = component * 32
        out_ref[:, pl.ds(start, 16, stride=2), :] = even_here.reshape(GROUPS, 16, LANES)
        out_ref[:, pl.ds(start + 1, 16, stride=2), :] = odd_here.reshape(GROUPS, 16, LANES)


def planes(metric, got, cosine, sine, cos_back, sin_back, forward):
    whole = pl.BlockSpec(memory_space=VMEM)
    return pl.pallas_call(
        plane_kernel,
        in_specs=[pl.BlockSpec(memory_space=SMEM)] + [whole] * 6,
        out_specs=whole,
        out_shape=jax.ShapeDtypeStruct((GROUPS, ROWS, LANES), F32),
        compiler_params=granted(20),
        cost_estimate=pl.CostEstimate(flops=3000000000, bytes_accessed=4000000, transcendentals=0),
        name="planes",
    )(metric, got, cosine, sine, cos_back, sin_back, forward)


def place_kernel(stator_ref, offset_ref, interp_ref, out_ref, base_ref, place_ref):
    for edge in range(32):
        rows = pl.ds(edge * 8, 8)
        base_ref[rows, :] = interp_ref[pl.ds(pl.multiple_of(offset_ref[edge] * 8, 8), 8), :]
        place_ref[rows, :] = jnp.full((8, 256), stator_ref[edge], jnp.int32)
    lane = lax.broadcasted_iota(jnp.int32, (256, 256), 1)
    high, low = split(jnp.where(place_ref[...] == lane // 8, base_ref[...], 0.0))
    out_ref[...] = jnp.concatenate([high, low, high], 0)


def placing(stator_element, mortar_offset, interp):
    scalars = pl.BlockSpec(memory_space=SMEM)
    whole = pl.BlockSpec(memory_space=VMEM)
    return pl.pallas_call(
        place_kernel,
        in_specs=[scalars, scalars, whole],
        out_specs=whole,
        out_shape=jax.ShapeDtypeStruct((768, 256), BF16),
        scratch_shapes=[pltpu.VMEM((256, 256), F32), pltpu.VMEM((256, 256), jnp.int32)],
        compiler_params=granted(4),
        cost_estimate=pl.CostEstimate(flops=1000, bytes_accessed=1000, transcendentals=0),
        name="placing",
    )(stator_element, mortar_offset, interp)


def penalty_kernel(source_ref, place_ref, *refs):
    piece_refs, (out_ref, received_ref) = refs[:HELD], refs[HELD:]
    elem = lax.axis_index("elem")
    core = elem % 2
    for edge in range(32):
        source = source_ref[edge]
        owner, slot = lax.shift_right_logical(source, 5), source & 31
        owner_core = owner & 1
        behind = (elem // 2 - lax.shift_right_logical(owner, 1)) & (RING - 1)
        near = jnp.where(behind <= 4, behind, RING - behind)
        side = jnp.where(
            behind == 0, core, jnp.where(behind == 4, owner_core, jnp.where(behind < 4, 0, 1))
        )
        piece = jnp.where((behind == 0) | (side == core), near, near + 4)
        first = pl.multiple_of(slot * 8, 8)
        start = pl.multiple_of((jnp.where(side == owner_core, 0, 32) + slot) * 8, 8)
        tile = piece_refs[0][pl.ds(start, 8), :]
        for index in range(1, HELD):
            at = first if index % 4 == 0 else start
            tile = jnp.where(piece == index, piece_refs[index][pl.ds(at, 8), :], tile)
        received_ref[pl.ds(edge * 8, 8), :] = tile
    out_ref[...] = dot(left_split(received_ref[...].T[:ROWS]), place_ref[...])


def penalty(stator_source, place, pieces):
    whole = pl.BlockSpec(memory_space=VMEM)
    return pl.pallas_call(
        penalty_kernel,
        in_specs=[pl.BlockSpec(memory_space=SMEM)] + [whole] * (HELD + 1),
        out_specs=whole,
        out_shape=jax.ShapeDtypeStruct((ROWS, 256), F32),
        scratch_shapes=[pltpu.VMEM((256, LANES), F32)],
        compiler_params=granted(6),
        cost_estimate=pl.CostEstimate(flops=1000, bytes_accessed=1000, transcendentals=0),
        name="penalty",
    )(stator_source, place, *pieces)


def sum_kernel(nonlinear_ref, helm_ref, placed_ref, out_ref, done_ref, sems):
    stores = [
        pltpu.make_async_copy(
            done_ref.at[block], out_ref.at[:, pl.ds(block * LANES, LANES)], sems.at[block]
        )
        for block in range(GROUPS)
    ]
    lane = lax.broadcasted_iota(jnp.int32, (ROWS, LANES), 1)
    for block in range(GROUPS):
        half = placed_ref[:, pl.ds((block // 8) * LANES, LANES)]
        start = 16 * (block % 8)
        low = pltpu.roll(half, (-start) % LANES, 1)
        high = pltpu.roll(half, (64 - 8 - start) % LANES, 1)
        value = jnp.where(lane < 8, low, jnp.where(lane // 8 == 8, high, 0.0))
        done_ref[block] = value - helm_ref[block] - nonlinear_ref[block]
        stores[block].start()
    for store in stores:
        store.wait()


def final_sum(nonlinear, helm, placed):
    whole = pl.BlockSpec(memory_space=VMEM)
    return pl.pallas_call(
        sum_kernel,
        in_specs=[whole] * 3,
        out_specs=pl.BlockSpec(memory_space=pl.ANY),
        out_shape=jax.ShapeDtypeStruct((ROWS, GROUPS * LANES), F32),
        scratch_shapes=[
            pltpu.VMEM((GROUPS, ROWS, LANES), F32),
            pltpu.SemaphoreType.DMA((GROUPS,)),
        ],
        compiler_params=granted(6),
        cost_estimate=pl.CostEstimate(flops=0, bytes_accessed=2400000, transcendentals=0),
        name="final_sum",
    )(nonlinear, helm, placed)


def local(vel_hat, metric, area, visc, rotor_element, stator_element, mortar_offset, stator_source):
    along_xi, along_eta, node_weight, interp = element_tables()
    cosine, sine, cos_back, sin_back = span_tables()
    forward = as_right(np.concatenate([along_xi.T, along_eta.T], 1))
    back = as_right(np.concatenate([along_xi, along_eta], 0))
    weight = jnp.asarray(np.tile(node_weight, 2)[None, :], F32)
    spread = np.tile(TAU_COEF * interp.transpose(0, 2, 1), (1, 1, 32))
    spread = jnp.asarray(spread.reshape(NQ * NQ, 256), F32)

    packed = pack(vel_hat.reshape(ROWS, GROUPS * LANES))
    got = lax.all_to_all(packed, "four", 0, 0, tiled=True)
    mine = traces(rotor_element, packed)
    both = pair(mine, lax.ppermute(mine, "elem", ACROSS))
    one = lax.ppermute(both, "elem", moves(1))
    two = lax.ppermute(both, "elem", moves(2))
    helm = helmholtz(
        metric, area, stator_element, packed, visc.reshape(GROUPS, LANES), weight, forward, back
    )
    place = placing(stator_element, mortar_offset, spread)
    got, helm = lax.optimization_barrier((got, helm))
    one, two = lax.optimization_barrier((one, two))
    advect_hat = planes(
        metric, got, as_left(cosine), as_left(sine), as_left(cos_back), as_left(sin_back), forward
    )
    nonlinear = lax.all_to_all(advect_hat, "four", 0, 0, tiled=True)
    three = lax.ppermute(two, "elem", moves(1))
    four = lax.ppermute(two[:256], "elem", moves(2))
    four, place = lax.optimization_barrier((four, place))
    held = [one, two, three, four]
    pieces = [both] + held + [lax.ppermute(piece, "elem", ACROSS) for piece in held]
    placed = penalty(stator_source, place, pieces)
    return final_sum(nonlinear, helm, placed).reshape(vel_hat.shape)


def solution(mesh):
    in_specs = (
        P(None, "four", "elem"),
        P(None, "elem"),
        P("elem"),
        P("elem"),
        P("elem"),
        P("elem"),
        P("elem"),
        P("elem"),
    )
    out_specs = P(None, "four", "elem")
    return jax.shard_map(local, mesh=mesh, in_specs=in_specs, out_specs=out_specs, check_vma=False)
```

```python
import math

import jax
import jax.numpy as jnp
import numpy as np
from jax import lax
from jax.experimental import pallas as pl
from jax.experimental.pallas import tpu as pltpu
from jax.sharding import PartitionSpec as P

NQ = 8
MODES = 512
PLANES = 768
HALF = PLANES // 2
PAIRS = MODES // 2
HELD = 9
RING = 8
GROUPS = 16
ROWS = 96
LANES = 128

LAMBDA_COEF = 10.0
TAU_COEF = 2.0
KZ_DIV = 32.0

F32 = jnp.float32
BF16 = jnp.bfloat16
VMEM = pltpu.MemorySpace.VMEM
SMEM = pltpu.MemorySpace.SMEM


def element_tables():
    order = NQ - 1
    points = -np.cos(np.pi * np.arange(NQ) / order)
    barycentric = np.array([(-1.0) ** index_a for index_a in range(NQ)])
    barycentric[0] *= 0.5
    barycentric[-1] *= 0.5
    derivative = np.zeros((NQ, NQ))
    for index_a in range(NQ):
        for index_b in range(NQ):
            if index_a != index_b:
                derivative[index_a, index_b] = (
                    barycentric[index_b]
                    / barycentric[index_a]
                    / (points[index_a] - points[index_b])
                )
        derivative[index_a, index_a] = -np.sum(derivative[index_a])
    angles = np.pi * np.arange(NQ) / order
    weights = np.ones(NQ)
    for harmonic in range(1, order // 2 + 1):
        weights = weights - 2.0 * np.cos(2 * harmonic * angles) / (4 * harmonic * harmonic - 1)
    weights = weights * 2.0 / order
    weights[0] *= 0.5
    weights[-1] *= 0.5
    identity = np.eye(NQ)
    along_xi = np.kron(np.eye(2), np.kron(identity, derivative))
    along_eta = np.kron(np.eye(2), np.kron(derivative, identity))
    node_weight = np.kron(weights, weights)
    interp = np.ones((NQ, NQ, NQ))
    for offset in range(NQ):
        targets = points * (1.0 - offset / 16.0) + offset / 16.0
        for index_a in range(NQ):
            for index_b in range(NQ):
                for index_c in range(NQ):
                    if index_c != index_b:
                        interp[offset, index_a, index_b] *= (targets[index_a] - points[index_c]) / (
                            points[index_b] - points[index_c]
                        )
    return along_xi, along_eta, node_weight, interp


def two_parts(table):
    table = np.asarray(table, np.float32)
    high = table.astype(BF16)
    low = (table - high.astype(np.float32)).astype(BF16)
    return high, low


def as_right(table):
    high, low = two_parts(table)
    return jnp.asarray(np.concatenate([high, low, high], 0))


def span_factors():
    other = np.arange(HALF)[None, :]
    factors = []
    for own in (16 * np.arange(HALF // 16)[:, None], np.arange(16)[:, None]):
        angle = 2.0 * np.pi * ((own * other) % PLANES) / PLANES
        factors += [jnp.asarray(np.cos(angle), F32), jnp.asarray(np.sin(angle), F32)]
    return factors


def granted(mebibytes):
    return pltpu.CompilerParams(vmem_limit_bytes=mebibytes * 1024 * 1024)


def split(value):
    high = value.astype(BF16)
    low = (value - high.astype(F32)).astype(BF16)
    return high, low


def dot(left, right):
    return jnp.dot(left, right, preferred_element_type=F32)


def left_split(value):
    high, low = split(value)
    return jnp.concatenate([high, high, low], -1)


def twice_high(table):
    return jnp.concatenate([table, table[:, : table.shape[1] // 2]], 1)


def right_split(value):
    high, low = split(value)
    return jnp.concatenate([high, high, low], 0)


def lane_scalars(first, second):
    lane = lax.broadcasted_iota(jnp.int32, (1, LANES), 1)
    return jnp.where(lane < LANES // 2, first, second)


def pack_kernel(field_ref, out_ref):
    for block in range(out_ref.shape[0]):
        out_ref[block] = field_ref[:, pl.ds(block * LANES, LANES)]


def pack(field):
    step = 8
    return pl.pallas_call(
        pack_kernel,
        grid=(GROUPS // step,),
        in_specs=[pl.BlockSpec((ROWS, step * LANES), lambda i: (0, i))],
        out_specs=pl.BlockSpec((step, ROWS, LANES), lambda i: (i, 0, 0)),
        out_shape=jax.ShapeDtypeStruct((GROUPS, ROWS, LANES), F32),
        compiler_params=granted(60),
        cost_estimate=pl.CostEstimate(flops=0, bytes_accessed=1600000, transcendentals=0),
        name="pack",
    )(field)


def trace_kernel(rotor_ref, packed_ref, out_ref, top_ref):
    lane = lax.broadcasted_iota(jnp.int32, (ROWS, LANES), 1)
    zeros = jnp.zeros((LANES - ROWS, LANES), F32)
    for half in range(2):
        rows = jnp.zeros((ROWS, LANES), F32)
        for block in range(8):
            field = packed_ref[half * 8 + block]
            low = pltpu.roll(field, (16 * block - 56) % LANES, 1)
            high = pltpu.roll(field, (16 * block + 8 - 120) % LANES, 1)
            rows = jnp.where(lane // 8 == 2 * block, low, rows)
            rows = jnp.where(lane // 8 == 2 * block + 1, high, rows)
        top_ref[pl.ds(half * LANES, LANES), :] = jnp.concatenate([rows, zeros], 0).T
    for slot in range(32):
        start = pl.multiple_of(rotor_ref[slot] * 8, 8)
        out_ref[pl.ds(slot * 8, 8), :] = top_ref[pl.ds(start, 8), :]


def traces(rotor_element, packed):
    return pl.pallas_call(
        trace_kernel,
        in_specs=[pl.BlockSpec(memory_space=SMEM), pl.BlockSpec(memory_space=VMEM)],
        out_specs=pl.BlockSpec(memory_space=VMEM),
        out_shape=jax.ShapeDtypeStruct((256, LANES), F32),
        scratch_shapes=[pltpu.VMEM((256, LANES), F32)],
        compiler_params=granted(4),
        cost_estimate=pl.CostEstimate(flops=0, bytes_accessed=8000000, transcendentals=0),
        name="traces",
    )(rotor_element, packed)


def pair_kernel(mine_ref, other_ref, out_ref):
    out_ref[pl.ds(0, 256), :] = mine_ref[...]
    out_ref[pl.ds(256, 256), :] = other_ref[...]


def pair(mine, other):
    whole = pl.BlockSpec(memory_space=VMEM)
    return pl.pallas_call(
        pair_kernel,
        in_specs=[whole, whole],
        out_specs=whole,
        out_shape=jax.ShapeDtypeStruct((512, LANES), F32),
        compiler_params=granted(2),
        cost_estimate=pl.CostEstimate(flops=0, bytes_accessed=1000000, transcendentals=0),
        name="pair",
    )(mine, other)


def moves(distance, cores=(0, 1)):
    return [
        (2 * z + c, 2 * ((z + (distance if c == 0 else -distance)) % RING) + c)
        for z in range(RING)
        for c in cores
    ]


ACROSS = [(i, i ^ 1) for i in range(2 * RING)]


def helm_kernel(
    metric_ref, area_ref, stator_ref, packed_ref, visc_ref, weight_ref, forward_ref, back_ref, out_ref,
    count_ref,
):
    step = packed_ref.shape[0]
    first = pl.program_id(0) * step

    @pl.when(pl.program_id(0) == 0)
    def _():
        for element in range(32):
            count_ref[element] = 0
        for edge in range(32):
            count_ref[stator_ref[edge]] = count_ref[stator_ref[edge]] + 1

    four = lax.axis_index("four")
    row = lax.broadcasted_iota(jnp.int32, (ROWS, LANES), 0)
    inner = row % 32
    number = jnp.where((inner == 1) & (four == 0), MODES // 2, four * 16 + inner // 2)
    wave = number.astype(F32) / KZ_DIV
    wave_sq = wave * wave
    lane = lax.broadcasted_iota(jnp.int32, (1, LANES), 1)
    bottom = lane % 64 < NQ
    field = packed_ref[...].reshape(step * ROWS, LANES)
    grads = dot(left_split(field), forward_ref[...])
    masses, fluxes = [], []
    for block in range(step):
        pair = (first + block) * 2
        rx, ry, sx, sy = [
            lane_scalars(metric_ref[i, pair], metric_ref[i, pair + 1]) for i in range(4)
        ]
        count = lane_scalars(count_ref[pair], count_ref[pair + 1]).astype(F32)
        own = jnp.where(bottom, TAU_COEF * count, 0.0)
        area = lane_scalars(area_ref[pair], area_ref[pair + 1])
        weight = area * weight_ref[...]
        viscous = weight * visc_ref[pl.ds(first + block, 1), :]
        rows = slice(block * ROWS, (block + 1) * ROWS)
        grad_xi, grad_eta = grads[rows, :LANES], grads[rows, LANES:]
        cross = viscous * (rx * sx + ry * sy)
        flux_xi = (viscous * (rx * rx + ry * ry)) * grad_xi + cross * grad_eta
        flux_eta = cross * grad_xi + (viscous * (sx * sx + sy * sy)) * grad_eta
        fluxes.append(jnp.concatenate([flux_xi, flux_eta], 1))
        masses.append((weight * LAMBDA_COEF + own + viscous * wave_sq) * field[rows])
    stiff = dot(left_split(jnp.concatenate(fluxes, 0)), back_ref[...])
    for block in range(step):
        out_ref[block] = masses[block] + stiff[block * ROWS : (block + 1) * ROWS]


def helmholtz(metric, area, stator_element, packed, visc, weight, forward, back):
    step = 4
    return pl.pallas_call(
        helm_kernel,
        grid=(GROUPS // step,),
        in_specs=[
            pl.BlockSpec(memory_space=SMEM),
            pl.BlockSpec(memory_space=SMEM),
            pl.BlockSpec(memory_space=SMEM),
            pl.BlockSpec((step, ROWS, LANES), lambda i: (i, 0, 0)),
            pl.BlockSpec((GROUPS, LANES), lambda i: (0, 0)),
            pl.BlockSpec((1, LANES), lambda i: (0, 0)),
            pl.BlockSpec((3 * LANES, 2 * LANES), lambda i: (0, 0)),
            pl.BlockSpec((6 * LANES, LANES), lambda i: (0, 0)),
        ],
        out_specs=pl.BlockSpec((step, ROWS, LANES), lambda i: (i, 0, 0)),
        out_shape=jax.ShapeDtypeStruct((GROUPS, ROWS, LANES), F32),
        scratch_shapes=[pltpu.SMEM((32,), jnp.int32)],
        compiler_params=granted(8),
        cost_estimate=pl.CostEstimate(flops=2000000000, bytes_accessed=8000000, transcendentals=0),
        name="helm",
    )(metric, area, stator_element, packed, visc, weight, forward, back)


def table_kernel(cos_far_ref, sin_far_ref, cos_near_ref, sin_near_ref, out_ref):
    row = lax.broadcasted_iota(jnp.int32, (16, HALF), 0)
    for back, count, width in ((False, HALF, PAIRS), (True, PAIRS, HALF)):
        near_cos, near_sin = cos_near_ref[:, pl.ds(0, width)], sin_near_ref[:, pl.ds(0, width)]
        for step in range(count // 16):
            far_cos = cos_far_ref[pl.ds(step, 1), pl.ds(0, width)]
            far_sin = sin_far_ref[pl.ds(step, 1), pl.ds(0, width)]
            cosine = far_cos * near_cos - far_sin * near_sin
            sine = far_sin * near_cos + far_cos * near_sin
            if back:
                half = (row == 0) & (step == 0)
                cosine = jnp.where(half, 1.0 / PLANES, 2.0 / PLANES) * cosine
                sine = (2.0 / PLANES) * sine
            rows = pl.ds((HALF if back else 0) + step * 16, 16)
            for index, part in enumerate(split(cosine) + split(sine)):
                out_ref[rows, pl.ds(index * width, width)] = part


def tables():
    whole = pl.BlockSpec(memory_space=VMEM)
    return pl.pallas_call(
        table_kernel,
        in_specs=[whole] * 4,
        out_specs=whole,
        out_shape=VMEM((HALF + PAIRS, 4 * HALF), BF16),
        compiler_params=granted(4),
        cost_estimate=pl.CostEstimate(flops=1000, bytes_accessed=1000, transcendentals=0),
        name="tables",
    )(*span_factors())


def plane_kernel(metric_ref, got_ref, table_ref, forward_ref, out_ref, done_ref, sems):
    pair = lax.axis_index("four") * 2
    rx, ry, sx, sy = [
        lane_scalars(metric_ref[i, pair], metric_ref[i, pair + 1]) for i in range(4)
    ]
    number = lax.broadcasted_iota(jnp.int32, (PAIRS, LANES), 0)
    wave = number.astype(F32) / KZ_DIV
    sign = jnp.where(number % 2 == 0, 1.0, -1.0).astype(F32)
    plane = lax.broadcasted_iota(jnp.int32, (HALF, LANES), 0)
    third = jnp.where(plane % 3 == 0, 1.0, -0.5).astype(F32)
    is_first = plane == 0
    evens, odds = [], []
    for component in range(3):
        start = component * 32
        evens.append(got_ref[:, pl.ds(start, 16, stride=2), :].reshape(PAIRS, LANES))
        odds.append(got_ref[:, pl.ds(start + 1, 16, stride=2), :].reshape(PAIRS, LANES))
    evens_z = [wave * odd for odd in odds]
    odds_z = [-wave * even for even in evens]
    last_cos = [odd[0:1] for odd in odds]
    even_all = jnp.concatenate(evens + evens_z, 1)
    odd_all = jnp.concatenate(odds + odds_z, 1)
    cos_part = dot(twice_high(table_ref[pl.ds(0, HALF), pl.ds(0, 2 * PAIRS)]), right_split(even_all))
    sin_part = dot(twice_high(table_ref[pl.ds(0, HALF), pl.ds(2 * PAIRS, 2 * PAIRS)]), right_split(odd_all))
    plus, minus = [], []
    for index in range(6):
        lanes = slice(index * LANES, (index + 1) * LANES)
        cos_here, sin_here = cos_part[:, lanes], sin_part[:, lanes]
        middle = jnp.sum(sign * (evens + evens_z)[index], 0, keepdims=True)
        if index < 3:
            cos_here = cos_here + third * last_cos[index]
            middle = middle + last_cos[index]
        plus.append(cos_here + sin_here)
        minus.append(jnp.where(is_first, middle, cos_here - sin_here))

    speeds = [
        (values[0] * rx + values[1] * ry, values[0] * sx + values[1] * sy, values)
        for values in (plus, minus)
    ]
    cos_back, sin_back = [
        twice_high(table_ref[pl.ds(HALF, PAIRS), pl.ds(start, 2 * HALF)]) for start in (0, 2 * HALF)
    ]
    scale = jnp.where(number == 0, 1.0 / PLANES, 2.0 / PLANES).astype(F32)
    stores = []
    for index, components in enumerate(((0, 1), (2,))):
        even_sum, odd_sum, middles = [], [], []
        for component in components:
            both = []
            for along_xi, along_eta, values in speeds:
                grads = dot(left_split(values[component]), forward_ref[...])
                both.append(
                    along_xi * grads[:, :LANES]
                    + along_eta * grads[:, LANES:]
                    + values[2] * values[3 + component]
                )
            middles.append(both[1][0:1])
            mirrored = jnp.where(is_first, 0.0, both[1])
            even_sum.append(both[0] + mirrored)
            odd_sum.append(both[0] - mirrored)
        even_out = dot(cos_back, right_split(jnp.concatenate(even_sum, 1)))
        odd_out = dot(sin_back, right_split(jnp.concatenate(odd_sum, 1)))
        for i, component in enumerate(components):
            lanes = slice(i * LANES, (i + 1) * LANES)
            even_here = even_out[:, lanes] + (scale * sign) * middles[i]
            last = (2.0 / PLANES) * (
                jnp.sum(third * even_sum[i], 0, keepdims=True) + middles[i]
            )
            odd_here = jnp.where(number == 0, last, odd_out[:, lanes])
            start = component * 32
            done_ref[:, pl.ds(start, 16, stride=2), :] = even_here.reshape(GROUPS, 16, LANES)
            done_ref[:, pl.ds(start + 1, 16, stride=2), :] = odd_here.reshape(GROUPS, 16, LANES)
        rows = pl.ds(components[0] * 32, len(components) * 32)
        store = pltpu.make_async_copy(done_ref.at[:, rows], out_ref.at[:, rows], sems.at[index])
        store.start()
        stores.append(store)
    for store in stores:
        store.wait()


def planes(metric, got, tables, forward):
    whole = pl.BlockSpec(memory_space=VMEM)
    return pl.pallas_call(
        plane_kernel,
        in_specs=[pl.BlockSpec(memory_space=SMEM)] + [whole] * 3,
        out_specs=pl.BlockSpec(memory_space=pl.ANY),
        out_shape=jax.ShapeDtypeStruct((GROUPS, ROWS, LANES), F32),
        scratch_shapes=[
            pltpu.VMEM((GROUPS, ROWS, LANES), F32),
            pltpu.SemaphoreType.DMA((2,)),
        ],
        compiler_params=granted(20),
        cost_estimate=pl.CostEstimate(flops=3000000000, bytes_accessed=4000000, transcendentals=0),
        name="planes",
    )(metric, got, tables, forward)


def place_kernel(stator_ref, offset_ref, interp_ref, out_ref, base_ref, place_ref):
    for edge in range(32):
        rows = pl.ds(edge * 8, 8)
        base_ref[rows, :] = interp_ref[pl.ds(pl.multiple_of(offset_ref[edge] * 8, 8), 8), :]
        place_ref[rows, :] = jnp.full((8, 256), stator_ref[edge], jnp.int32)
    lane = lax.broadcasted_iota(jnp.int32, (256, 256), 1)
    high, low = split(jnp.where(place_ref[...] == lane // 8, base_ref[...], 0.0))
    out_ref[...] = jnp.concatenate([high, low, high], 0)


def placing(stator_element, mortar_offset, interp):
    scalars = pl.BlockSpec(memory_space=SMEM)
    whole = pl.BlockSpec(memory_space=VMEM)
    return pl.pallas_call(
        place_kernel,
        in_specs=[scalars, scalars, whole],
        out_specs=whole,
        out_shape=jax.ShapeDtypeStruct((768, 256), BF16),
        scratch_shapes=[pltpu.VMEM((256, 256), F32), pltpu.VMEM((256, 256), jnp.int32)],
        compiler_params=granted(4),
        cost_estimate=pl.CostEstimate(flops=1000, bytes_accessed=1000, transcendentals=0),
        name="placing",
    )(stator_element, mortar_offset, interp)


def penalty_kernel(source_ref, place_ref, *refs):
    piece_refs, (out_ref, received_ref) = refs[:HELD], refs[HELD:]
    elem = lax.axis_index("elem")
    core = elem % 2
    for edge in range(32):
        source = source_ref[edge]
        owner, slot = lax.shift_right_logical(source, 5), source & 31
        owner_core = owner & 1
        behind = (elem // 2 - lax.shift_right_logical(owner, 1)) & (RING - 1)
        near = jnp.where(behind <= 4, behind, RING - behind)
        side = jnp.where(
            behind == 0, core, jnp.where(behind == 4, owner_core, jnp.where(behind < 4, 0, 1))
        )
        piece = jnp.where((behind == 0) | (side == core), near, near + 4)
        first = pl.multiple_of(slot * 8, 8)
        start = pl.multiple_of((jnp.where(side == owner_core, 0, 32) + slot) * 8, 8)
        tile = piece_refs[0][pl.ds(start, 8), :]
        for index in range(1, HELD):
            at = first if index % 4 == 0 else start
            tile = jnp.where(piece == index, piece_refs[index][pl.ds(at, 8), :], tile)
        received_ref[pl.ds(edge * 8, 8), :] = tile
    out_ref[...] = dot(left_split(received_ref[...].T[:ROWS]), place_ref[...])


def penalty(stator_source, place, pieces):
    whole = pl.BlockSpec(memory_space=VMEM)
    return pl.pallas_call(
        penalty_kernel,
        in_specs=[pl.BlockSpec(memory_space=SMEM)] + [whole] * (HELD + 1),
        out_specs=whole,
        out_shape=jax.ShapeDtypeStruct((ROWS, 256), F32),
        scratch_shapes=[pltpu.VMEM((256, LANES), F32)],
        compiler_params=granted(6),
        cost_estimate=pl.CostEstimate(flops=1000, bytes_accessed=1000, transcendentals=0),
        name="penalty",
    )(stator_source, place, *pieces)


def sum_kernel(nonlinear_ref, helm_ref, placed_ref, out_ref, done_ref, sems):
    stores = [
        pltpu.make_async_copy(
            done_ref.at[block], out_ref.at[:, pl.ds(block * LANES, LANES)], sems.at[block]
        )
        for block in range(GROUPS)
    ]
    lane = lax.broadcasted_iota(jnp.int32, (ROWS, LANES), 1)
    for block in range(GROUPS):
        half = placed_ref[:, pl.ds((block // 8) * LANES, LANES)]
        start = 16 * (block % 8)
        low = pltpu.roll(half, (-start) % LANES, 1)
        high = pltpu.roll(half, (64 - 8 - start) % LANES, 1)
        value = jnp.where(lane < 8, low, jnp.where(lane // 8 == 8, high, 0.0))
        done_ref[block] = value - helm_ref[block] - nonlinear_ref[block]
        stores[block].start()
    for store in stores:
        store.wait()


def final_sum(nonlinear, helm, placed):
    whole = pl.BlockSpec(memory_space=VMEM)
    return pl.pallas_call(
        sum_kernel,
        in_specs=[whole] * 3,
        out_specs=pl.BlockSpec(memory_space=pl.ANY),
        out_shape=jax.ShapeDtypeStruct((ROWS, GROUPS * LANES), F32),
        scratch_shapes=[
            pltpu.VMEM((GROUPS, ROWS, LANES), F32),
            pltpu.SemaphoreType.DMA((GROUPS,)),
        ],
        compiler_params=granted(6),
        cost_estimate=pl.CostEstimate(flops=0, bytes_accessed=2400000, transcendentals=0),
        name="final_sum",
    )(nonlinear, helm, placed)


def local(vel_hat, metric, area, visc, rotor_element, stator_element, mortar_offset, stator_source):
    along_xi, along_eta, node_weight, interp = element_tables()
    forward = as_right(np.concatenate([along_xi.T, along_eta.T], 1))
    back = as_right(np.concatenate([along_xi, along_eta], 0))
    weight = jnp.asarray(np.tile(node_weight, 2)[None, :], F32)
    spread = np.tile(TAU_COEF * interp.transpose(0, 2, 1), (1, 1, 32))
    spread = jnp.asarray(spread.reshape(NQ * NQ, 256), F32)

    packed = pack(vel_hat.reshape(ROWS, GROUPS * LANES))
    got = lax.all_to_all(packed, "four", 0, 0, tiled=True)
    mine = traces(rotor_element, packed)
    both = pair(mine, lax.ppermute(mine, "elem", ACROSS))
    one = lax.ppermute(both, "elem", moves(1))
    three = lax.ppermute(both, "elem", moves(3))
    helm = helmholtz(
        metric, area, stator_element, packed, visc.reshape(GROUPS, LANES), weight, forward, back
    )
    place = placing(stator_element, mortar_offset, spread)
    table = tables()
    got, helm, table = lax.optimization_barrier((got, helm, table))
    one, three, place = lax.optimization_barrier((one, three, place))
    advect_hat = planes(metric, got, table, forward)
    nonlinear = lax.all_to_all(advect_hat, "four", 0, 0, tiled=True)
    two = lax.ppermute(one, "elem", moves(1))
    four = lax.ppermute(three[:256], "elem", moves(1))
    held = [one, two, three, four]
    pieces = [both] + held + [lax.ppermute(piece, "elem", ACROSS) for piece in held]
    placed = penalty(stator_source, place, pieces)
    return final_sum(nonlinear, helm, placed).reshape(vel_hat.shape)


def solution(mesh):
    in_specs = (
        P(None, "four", "elem"),
        P(None, "elem"),
        P("elem"),
        P("elem"),
        P("elem"),
        P("elem"),
        P("elem"),
        P("elem"),
    )
    out_specs = P(None, "four", "elem")
    return jax.shard_map(local, mesh=mesh, in_specs=in_specs, out_specs=out_specs, check_vma=False)
```

```python
import math

import jax
import jax.numpy as jnp
import numpy as np
from jax import lax
from jax.experimental import pallas as pl
from jax.experimental.pallas import tpu as pltpu
from jax.sharding import PartitionSpec as P

NQ = 8
MODES = 512
PLANES = 768
HALF = PLANES // 2
PAIRS = MODES // 2
HELD = 9
RING = 8
GROUPS = 16
ROWS = 96
LANES = 128

LAMBDA_COEF = 10.0
TAU_COEF = 2.0
KZ_DIV = 32.0

F32 = jnp.float32
BF16 = jnp.bfloat16
VMEM = pltpu.MemorySpace.VMEM
SMEM = pltpu.MemorySpace.SMEM


def element_tables():
    order = NQ - 1
    points = -np.cos(np.pi * np.arange(NQ) / order)
    barycentric = np.array([(-1.0) ** index_a for index_a in range(NQ)])
    barycentric[0] *= 0.5
    barycentric[-1] *= 0.5
    derivative = np.zeros((NQ, NQ))
    for index_a in range(NQ):
        for index_b in range(NQ):
            if index_a != index_b:
                derivative[index_a, index_b] = (
                    barycentric[index_b]
                    / barycentric[index_a]
                    / (points[index_a] - points[index_b])
                )
        derivative[index_a, index_a] = -np.sum(derivative[index_a])
    angles = np.pi * np.arange(NQ) / order
    weights = np.ones(NQ)
    for harmonic in range(1, order // 2 + 1):
        weights = weights - 2.0 * np.cos(2 * harmonic * angles) / (4 * harmonic * harmonic - 1)
    weights = weights * 2.0 / order
    weights[0] *= 0.5
    weights[-1] *= 0.5
    identity = np.eye(NQ)
    along_xi = np.kron(np.eye(2), np.kron(identity, derivative))
    along_eta = np.kron(np.eye(2), np.kron(derivative, identity))
    node_weight = np.kron(weights, weights)
    interp = np.ones((NQ, NQ, NQ))
    for offset in range(NQ):
        targets = points * (1.0 - offset / 16.0) + offset / 16.0
        for index_a in range(NQ):
            for index_b in range(NQ):
                for index_c in range(NQ):
                    if index_c != index_b:
                        interp[offset, index_a, index_b] *= (targets[index_a] - points[index_c]) / (
                            points[index_b] - points[index_c]
                        )
    return along_xi, along_eta, node_weight, interp


def two_parts(table):
    table = np.asarray(table, np.float32)
    high = table.astype(BF16)
    low = (table - high.astype(np.float32)).astype(BF16)
    return high, low


def as_right(table):
    high, low = two_parts(table)
    return jnp.asarray(np.concatenate([high, low, high], 0))


def span_factors():
    other = np.arange(HALF)[None, :]
    factors = []
    for own in (16 * np.arange(HALF // 16)[:, None], np.arange(16)[:, None]):
        angle = 2.0 * np.pi * ((own * other) % PLANES) / PLANES
        factors += [jnp.asarray(np.cos(angle), F32), jnp.asarray(np.sin(angle), F32)]
    return factors


def granted(mebibytes):
    return pltpu.CompilerParams(vmem_limit_bytes=mebibytes * 1024 * 1024)


def split(value):
    high = value.astype(BF16)
    low = (value - high.astype(F32)).astype(BF16)
    return high, low


def dot(left, right):
    return jnp.dot(left, right, preferred_element_type=F32)


def left_split(value):
    high, low = split(value)
    return jnp.concatenate([high, high, low], -1)


def twice_high(table):
    return jnp.concatenate([table, table[:, : table.shape[1] // 2]], 1)


def right_split(value):
    high, low = split(value)
    return jnp.concatenate([high, high, low], 0)


def lane_scalars(first, second):
    lane = lax.broadcasted_iota(jnp.int32, (1, LANES), 1)
    return jnp.where(lane < LANES // 2, first, second)


def pack_kernel(field_ref, out_ref):
    for block in range(out_ref.shape[0]):
        out_ref[block] = field_ref[:, pl.ds(block * LANES, LANES)]


def pack(field):
    step = 8
    return pl.pallas_call(
        pack_kernel,
        grid=(GROUPS // step,),
        in_specs=[pl.BlockSpec((ROWS, step * LANES), lambda i: (0, i))],
        out_specs=pl.BlockSpec((step, ROWS, LANES), lambda i: (i, 0, 0)),
        out_shape=jax.ShapeDtypeStruct((GROUPS, ROWS, LANES), F32),
        compiler_params=granted(60),
        cost_estimate=pl.CostEstimate(flops=0, bytes_accessed=1600000, transcendentals=0),
        name="pack",
    )(field)


def trace_kernel(rotor_ref, packed_ref, out_ref, top_ref):
    lane = lax.broadcasted_iota(jnp.int32, (ROWS, LANES), 1)
    zeros = jnp.zeros((LANES - ROWS, LANES), F32)
    for half in range(2):
        rows = jnp.zeros((ROWS, LANES), F32)
        for block in range(8):
            field = packed_ref[half * 8 + block]
            low = pltpu.roll(field, (16 * block - 56) % LANES, 1)
            high = pltpu.roll(field, (16 * block + 8 - 120) % LANES, 1)
            rows = jnp.where(lane // 8 == 2 * block, low, rows)
            rows = jnp.where(lane // 8 == 2 * block + 1, high, rows)
        top_ref[pl.ds(half * LANES, LANES), :] = jnp.concatenate([rows, zeros], 0).T
    for slot in range(32):
        start = pl.multiple_of(rotor_ref[slot] * 8, 8)
        out_ref[pl.ds(slot * 8, 8), :] = top_ref[pl.ds(start, 8), :]


def traces(rotor_element, packed):
    return pl.pallas_call(
        trace_kernel,
        in_specs=[pl.BlockSpec(memory_space=SMEM), pl.BlockSpec(memory_space=VMEM)],
        out_specs=pl.BlockSpec(memory_space=VMEM),
        out_shape=jax.ShapeDtypeStruct((256, LANES), F32),
        scratch_shapes=[pltpu.VMEM((256, LANES), F32)],
        compiler_params=granted(4),
        cost_estimate=pl.CostEstimate(flops=0, bytes_accessed=8000000, transcendentals=0),
        name="traces",
    )(rotor_element, packed)


def pair_kernel(mine_ref, other_ref, out_ref):
    out_ref[pl.ds(0, 256), :] = mine_ref[...]
    out_ref[pl.ds(256, 256), :] = other_ref[...]


def pair(mine, other):
    whole = pl.BlockSpec(memory_space=VMEM)
    return pl.pallas_call(
        pair_kernel,
        in_specs=[whole, whole],
        out_specs=whole,
        out_shape=jax.ShapeDtypeStruct((512, LANES), F32),
        compiler_params=granted(2),
        cost_estimate=pl.CostEstimate(flops=0, bytes_accessed=1000000, transcendentals=0),
        name="pair",
    )(mine, other)


def moves(distance, cores=(0, 1)):
    return [
        (2 * z + c, 2 * ((z + (distance if c == 0 else -distance)) % RING) + c)
        for z in range(RING)
        for c in cores
    ]


ACROSS = [(i, i ^ 1) for i in range(2 * RING)]


def helm_kernel(
    metric_ref, area_ref, stator_ref, packed_ref, visc_ref, weight_ref, forward_ref, back_ref, out_ref,
    count_ref,
):
    step = packed_ref.shape[0]
    first = pl.program_id(0) * step

    @pl.when(pl.program_id(0) == 0)
    def _():
        for element in range(32):
            count_ref[element] = 0
        for edge in range(32):
            count_ref[stator_ref[edge]] = count_ref[stator_ref[edge]] + 1

    four = lax.axis_index("four")
    row = lax.broadcasted_iota(jnp.int32, (ROWS, LANES), 0)
    inner = row % 32
    number = jnp.where((inner == 1) & (four == 0), MODES // 2, four * 16 + inner // 2)
    wave = number.astype(F32) / KZ_DIV
    wave_sq = wave * wave
    lane = lax.broadcasted_iota(jnp.int32, (1, LANES), 1)
    bottom = lane % 64 < NQ
    field = packed_ref[...].reshape(step * ROWS, LANES)
    grads = dot(left_split(field), forward_ref[...])
    masses, fluxes = [], []
    for block in range(step):
        pair = (first + block) * 2
        rx, ry, sx, sy = [
            lane_scalars(metric_ref[i, pair], metric_ref[i, pair + 1]) for i in range(4)
        ]
        count = lane_scalars(count_ref[pair], count_ref[pair + 1]).astype(F32)
        own = jnp.where(bottom, TAU_COEF * count, 0.0)
        area = lane_scalars(area_ref[pair], area_ref[pair + 1])
        weight = area * weight_ref[...]
        viscous = weight * visc_ref[pl.ds(first + block, 1), :]
        rows = slice(block * ROWS, (block + 1) * ROWS)
        grad_xi, grad_eta = grads[rows, :LANES], grads[rows, LANES:]
        cross = viscous * (rx * sx + ry * sy)
        flux_xi = (viscous * (rx * rx + ry * ry)) * grad_xi + cross * grad_eta
        flux_eta = cross * grad_xi + (viscous * (sx * sx + sy * sy)) * grad_eta
        fluxes.append(jnp.concatenate([flux_xi, flux_eta], 1))
        masses.append((weight * LAMBDA_COEF + own + viscous * wave_sq) * field[rows])
    stiff = dot(left_split(jnp.concatenate(fluxes, 0)), back_ref[...])
    for block in range(step):
        out_ref[block] = masses[block] + stiff[block * ROWS : (block + 1) * ROWS]


def helmholtz(metric, area, stator_element, packed, visc, weight, forward, back):
    step = 4
    return pl.pallas_call(
        helm_kernel,
        grid=(GROUPS // step,),
        in_specs=[
            pl.BlockSpec(memory_space=SMEM),
            pl.BlockSpec(memory_space=SMEM),
            pl.BlockSpec(memory_space=SMEM),
            pl.BlockSpec((step, ROWS, LANES), lambda i: (i, 0, 0)),
            pl.BlockSpec((GROUPS, LANES), lambda i: (0, 0)),
            pl.BlockSpec((1, LANES), lambda i: (0, 0)),
            pl.BlockSpec((3 * LANES, 2 * LANES), lambda i: (0, 0)),
            pl.BlockSpec((6 * LANES, LANES), lambda i: (0, 0)),
        ],
        out_specs=pl.BlockSpec((step, ROWS, LANES), lambda i: (i, 0, 0)),
        out_shape=jax.ShapeDtypeStruct((GROUPS, ROWS, LANES), F32),
        scratch_shapes=[pltpu.SMEM((32,), jnp.int32)],
        compiler_params=granted(8),
        cost_estimate=pl.CostEstimate(flops=2000000000, bytes_accessed=8000000, transcendentals=0),
        name="helm",
    )(metric, area, stator_element, packed, visc, weight, forward, back)


def make_tables(back, factors, table_ref):
    count, width = (PAIRS, HALF) if back else (HALF, PAIRS)
    cos_far_ref, sin_far_ref, cos_near_ref, sin_near_ref = factors
    near_cos, near_sin = cos_near_ref[:, pl.ds(0, width)], sin_near_ref[:, pl.ds(0, width)]
    row = lax.broadcasted_iota(jnp.int32, (16, width), 0)
    for step in range(count // 16):
        far_cos = cos_far_ref[pl.ds(step, 1), pl.ds(0, width)]
        far_sin = sin_far_ref[pl.ds(step, 1), pl.ds(0, width)]
        cosine = far_cos * near_cos - far_sin * near_sin
        sine = far_sin * near_cos + far_cos * near_sin
        if back:
            half = (row == 0) & (step == 0)
            cosine = jnp.where(half, 1.0 / PLANES, 2.0 / PLANES) * cosine
            sine = (2.0 / PLANES) * sine
        rows = pl.ds((HALF if back else 0) + step * 16, 16)
        for index, part in enumerate(split(cosine) + split(sine)):
            table_ref[rows, pl.ds(index * width, width)] = part


def plane_kernel(metric_ref, got_ref, forward_ref, *refs):
    factors, (out_ref, table_ref, done_ref, sems) = refs[:4], refs[4:]
    make_tables(False, factors, table_ref)
    make_tables(True, factors, table_ref)
    pair = lax.axis_index("four") * 2
    rx, ry, sx, sy = [
        lane_scalars(metric_ref[i, pair], metric_ref[i, pair + 1]) for i in range(4)
    ]
    number = lax.broadcasted_iota(jnp.int32, (PAIRS, LANES), 0)
    wave = number.astype(F32) / KZ_DIV
    sign = jnp.where(number % 2 == 0, 1.0, -1.0).astype(F32)
    plane = lax.broadcasted_iota(jnp.int32, (HALF, LANES), 0)
    third = jnp.where(plane % 3 == 0, 1.0, -0.5).astype(F32)
    is_first = plane == 0
    evens, odds = [], []
    for component in range(3):
        start = component * 32
        evens.append(got_ref[:, pl.ds(start, 16, stride=2), :].reshape(PAIRS, LANES))
        odds.append(got_ref[:, pl.ds(start + 1, 16, stride=2), :].reshape(PAIRS, LANES))
    evens_z = [wave * odd for odd in odds]
    odds_z = [-wave * even for even in evens]
    last_cos = [odd[0:1] for odd in odds]
    even_all = jnp.concatenate(evens + evens_z, 1)
    odd_all = jnp.concatenate(odds + odds_z, 1)
    cos_part = dot(twice_high(table_ref[pl.ds(0, HALF), pl.ds(0, 2 * PAIRS)]), right_split(even_all))
    sin_part = dot(twice_high(table_ref[pl.ds(0, HALF), pl.ds(2 * PAIRS, 2 * PAIRS)]), right_split(odd_all))
    plus, minus = [], []
    for index in range(6):
        lanes = slice(index * LANES, (index + 1) * LANES)
        cos_here, sin_here = cos_part[:, lanes], sin_part[:, lanes]
        middle = jnp.sum(sign * (evens + evens_z)[index], 0, keepdims=True)
        if index < 3:
            cos_here = cos_here + third * last_cos[index]
            middle = middle + last_cos[index]
        plus.append(cos_here + sin_here)
        minus.append(jnp.where(is_first, middle, cos_here - sin_here))

    speeds = [
        (values[0] * rx + values[1] * ry, values[0] * sx + values[1] * sy, values)
        for values in (plus, minus)
    ]
    cos_back, sin_back = [
        twice_high(table_ref[pl.ds(HALF, PAIRS), pl.ds(start, 2 * HALF)]) for start in (0, 2 * HALF)
    ]
    scale = jnp.where(number == 0, 1.0 / PLANES, 2.0 / PLANES).astype(F32)
    stores = []
    for index, components in enumerate(((0, 1), (2,))):
        even_sum, odd_sum, middles = [], [], []
        for component in components:
            both = []
            for along_xi, along_eta, values in speeds:
                grads = dot(left_split(values[component]), forward_ref[...])
                both.append(
                    along_xi * grads[:, :LANES]
                    + along_eta * grads[:, LANES:]
                    + values[2] * values[3 + component]
                )
            middles.append(both[1][0:1])
            mirrored = jnp.where(is_first, 0.0, both[1])
            even_sum.append(both[0] + mirrored)
            odd_sum.append(both[0] - mirrored)
        even_out = dot(cos_back, right_split(jnp.concatenate(even_sum, 1)))
        odd_out = dot(sin_back, right_split(jnp.concatenate(odd_sum, 1)))
        for i, component in enumerate(components):
            lanes = slice(i * LANES, (i + 1) * LANES)
            even_here = even_out[:, lanes] + (scale * sign) * middles[i]
            last = (2.0 / PLANES) * (
                jnp.sum(third * even_sum[i], 0, keepdims=True) + middles[i]
            )
            odd_here = jnp.where(number == 0, last, odd_out[:, lanes])
            start = component * 32
            done_ref[:, pl.ds(start, 16, stride=2), :] = even_here.reshape(GROUPS, 16, LANES)
            done_ref[:, pl.ds(start + 1, 16, stride=2), :] = odd_here.reshape(GROUPS, 16, LANES)
        rows = pl.ds(components[0] * 32, len(components) * 32)
        store = pltpu.make_async_copy(done_ref.at[:, rows], out_ref.at[:, rows], sems.at[index])
        store.start()
        stores.append(store)
    for store in stores:
        store.wait()


def planes(metric, got, factors, forward):
    whole = pl.BlockSpec(memory_space=VMEM)
    return pl.pallas_call(
        plane_kernel,
        in_specs=[pl.BlockSpec(memory_space=SMEM)] + [whole] * 6,
        out_specs=pl.BlockSpec(memory_space=pl.ANY),
        out_shape=jax.ShapeDtypeStruct((GROUPS, ROWS, LANES), F32),
        scratch_shapes=[
            pltpu.VMEM((HALF + PAIRS, 4 * HALF), BF16),
            pltpu.VMEM((GROUPS, ROWS, LANES), F32),
            pltpu.SemaphoreType.DMA((2,)),
        ],
        compiler_params=granted(20),
        cost_estimate=pl.CostEstimate(flops=3000000000, bytes_accessed=4000000, transcendentals=0),
        name="planes",
    )(metric, got, forward, *factors)


def place_kernel(stator_ref, offset_ref, interp_ref, out_ref, base_ref, place_ref):
    for edge in range(32):
        rows = pl.ds(edge * 8, 8)
        base_ref[rows, :] = interp_ref[pl.ds(pl.multiple_of(offset_ref[edge] * 8, 8), 8), :]
        place_ref[rows, :] = jnp.full((8, 256), stator_ref[edge], jnp.int32)
    lane = lax.broadcasted_iota(jnp.int32, (256, 256), 1)
    high, low = split(jnp.where(place_ref[...] == lane // 8, base_ref[...], 0.0))
    out_ref[...] = jnp.concatenate([high, low, high], 0)


def placing(stator_element, mortar_offset, interp):
    scalars = pl.BlockSpec(memory_space=SMEM)
    whole = pl.BlockSpec(memory_space=VMEM)
    return pl.pallas_call(
        place_kernel,
        in_specs=[scalars, scalars, whole],
        out_specs=whole,
        out_shape=jax.ShapeDtypeStruct((768, 256), BF16),
        scratch_shapes=[pltpu.VMEM((256, 256), F32), pltpu.VMEM((256, 256), jnp.int32)],
        compiler_params=granted(4),
        cost_estimate=pl.CostEstimate(flops=1000, bytes_accessed=1000, transcendentals=0),
        name="placing",
    )(stator_element, mortar_offset, interp)


def penalty_kernel(source_ref, place_ref, *refs):
    piece_refs, (out_ref, received_ref) = refs[:HELD], refs[HELD:]
    elem = lax.axis_index("elem")
    core = elem % 2
    for edge in range(32):
        source = source_ref[edge]
        owner, slot = lax.shift_right_logical(source, 5), source & 31
        owner_core = owner & 1
        behind = (elem // 2 - lax.shift_right_logical(owner, 1)) & (RING - 1)
        near = jnp.where(behind <= 4, behind, RING - behind)
        side = jnp.where(
            behind == 0, core, jnp.where(behind == 4, owner_core, jnp.where(behind < 4, 0, 1))
        )
        piece = jnp.where((behind == 0) | (side == core), near, near + 4)
        first = pl.multiple_of(slot * 8, 8)
        start = pl.multiple_of((jnp.where(side == owner_core, 0, 32) + slot) * 8, 8)
        tile = piece_refs[0][pl.ds(start, 8), :]
        for index in range(1, HELD):
            at = first if index % 4 == 0 else start
            tile = jnp.where(piece == index, piece_refs[index][pl.ds(at, 8), :], tile)
        received_ref[pl.ds(edge * 8, 8), :] = tile
    out_ref[...] = dot(left_split(received_ref[...].T[:ROWS]), place_ref[...])


def penalty(stator_source, place, pieces):
    whole = pl.BlockSpec(memory_space=VMEM)
    return pl.pallas_call(
        penalty_kernel,
        in_specs=[pl.BlockSpec(memory_space=SMEM)] + [whole] * (HELD + 1),
        out_specs=whole,
        out_shape=jax.ShapeDtypeStruct((ROWS, 256), F32),
        scratch_shapes=[pltpu.VMEM((256, LANES), F32)],
        compiler_params=granted(6),
        cost_estimate=pl.CostEstimate(flops=1000, bytes_accessed=1000, transcendentals=0),
        name="penalty",
    )(stator_source, place, *pieces)


def sum_kernel(nonlinear_ref, helm_ref, placed_ref, out_ref, done_ref, sems):
    stores = [
        pltpu.make_async_copy(
            done_ref.at[block], out_ref.at[:, pl.ds(block * LANES, LANES)], sems.at[block]
        )
        for block in range(GROUPS)
    ]
    lane = lax.broadcasted_iota(jnp.int32, (ROWS, LANES), 1)
    for block in range(GROUPS):
        half = placed_ref[:, pl.ds((block // 8) * LANES, LANES)]
        start = 16 * (block % 8)
        low = pltpu.roll(half, (-start) % LANES, 1)
        high = pltpu.roll(half, (64 - 8 - start) % LANES, 1)
        value = jnp.where(lane < 8, low, jnp.where(lane // 8 == 8, high, 0.0))
        done_ref[block] = value - helm_ref[block] - nonlinear_ref[block]
        stores[block].start()
    for store in stores:
        store.wait()


def final_sum(nonlinear, helm, placed):
    whole = pl.BlockSpec(memory_space=VMEM)
    return pl.pallas_call(
        sum_kernel,
        in_specs=[whole] * 3,
        out_specs=pl.BlockSpec(memory_space=pl.ANY),
        out_shape=jax.ShapeDtypeStruct((ROWS, GROUPS * LANES), F32),
        scratch_shapes=[
            pltpu.VMEM((GROUPS, ROWS, LANES), F32),
            pltpu.SemaphoreType.DMA((GROUPS,)),
        ],
        compiler_params=granted(6),
        cost_estimate=pl.CostEstimate(flops=0, bytes_accessed=2400000, transcendentals=0),
        name="final_sum",
    )(nonlinear, helm, placed)


def local(vel_hat, metric, area, visc, rotor_element, stator_element, mortar_offset, stator_source):
    along_xi, along_eta, node_weight, interp = element_tables()
    forward = as_right(np.concatenate([along_xi.T, along_eta.T], 1))
    back = as_right(np.concatenate([along_xi, along_eta], 0))
    weight = jnp.asarray(np.tile(node_weight, 2)[None, :], F32)
    spread = np.tile(TAU_COEF * interp.transpose(0, 2, 1), (1, 1, 32))
    spread = jnp.asarray(spread.reshape(NQ * NQ, 256), F32)

    packed = pack(vel_hat.reshape(ROWS, GROUPS * LANES))
    got = lax.all_to_all(packed, "four", 0, 0, tiled=True)
    mine = traces(rotor_element, packed)
    both = pair(mine, lax.ppermute(mine, "elem", ACROSS))
    one = lax.ppermute(both, "elem", moves(1))
    three = lax.ppermute(both, "elem", moves(3))
    helm = helmholtz(
        metric, area, stator_element, packed, visc.reshape(GROUPS, LANES), weight, forward, back
    )
    place = placing(stator_element, mortar_offset, spread)
    got, helm = lax.optimization_barrier((got, helm))
    one, three = lax.optimization_barrier((one, three))
    advect_hat = planes(metric, got, span_factors(), forward)
    nonlinear = lax.all_to_all(advect_hat, "four", 0, 0, tiled=True)
    two = lax.ppermute(one, "elem", moves(1))
    four = lax.ppermute(three[:256], "elem", moves(1))
    four, place = lax.optimization_barrier((four, place))
    held = [one, two, three, four]
    pieces = [both] + held + [lax.ppermute(piece, "elem", ACROSS) for piece in held]
    placed = penalty(stator_source, place, pieces)
    return final_sum(nonlinear, helm, placed).reshape(vel_hat.shape)


def solution(mesh):
    in_specs = (
        P(None, "four", "elem"),
        P(None, "elem"),
        P("elem"),
        P("elem"),
        P("elem"),
        P("elem"),
        P("elem"),
        P("elem"),
    )
    out_specs = P(None, "four", "elem")
    return jax.shard_map(local, mesh=mesh, in_specs=in_specs, out_specs=out_specs, check_vma=False)
```

```python
import math

import jax
import jax.numpy as jnp
import numpy as np
from jax import lax
from jax.experimental import pallas as pl
from jax.experimental.pallas import tpu as pltpu
from jax.sharding import PartitionSpec as P

NQ = 8
MODES = 512
PLANES = 768
HALF = PLANES // 2
PAIRS = MODES // 2
HELD = 9
RING = 8
GROUPS = 16
ROWS = 96
LANES = 128

LAMBDA_COEF = 10.0
TAU_COEF = 2.0
KZ_DIV = 32.0

F32 = jnp.float32
BF16 = jnp.bfloat16
VMEM = pltpu.MemorySpace.VMEM
SMEM = pltpu.MemorySpace.SMEM


def element_tables():
    order = NQ - 1
    points = -np.cos(np.pi * np.arange(NQ) / order)
    barycentric = np.array([(-1.0) ** index_a for index_a in range(NQ)])
    barycentric[0] *= 0.5
    barycentric[-1] *= 0.5
    derivative = np.zeros((NQ, NQ))
    for index_a in range(NQ):
        for index_b in range(NQ):
            if index_a != index_b:
                derivative[index_a, index_b] = (
                    barycentric[index_b]
                    / barycentric[index_a]
                    / (points[index_a] - points[index_b])
                )
        derivative[index_a, index_a] = -np.sum(derivative[index_a])
    angles = np.pi * np.arange(NQ) / order
    weights = np.ones(NQ)
    for harmonic in range(1, order // 2 + 1):
        weights = weights - 2.0 * np.cos(2 * harmonic * angles) / (4 * harmonic * harmonic - 1)
    weights = weights * 2.0 / order
    weights[0] *= 0.5
    weights[-1] *= 0.5
    identity = np.eye(NQ)
    along_xi = np.kron(np.eye(2), np.kron(identity, derivative))
    along_eta = np.kron(np.eye(2), np.kron(derivative, identity))
    node_weight = np.kron(weights, weights)
    interp = np.ones((NQ, NQ, NQ))
    for offset in range(NQ):
        targets = points * (1.0 - offset / 16.0) + offset / 16.0
        for index_a in range(NQ):
            for index_b in range(NQ):
                for index_c in range(NQ):
                    if index_c != index_b:
                        interp[offset, index_a, index_b] *= (targets[index_a] - points[index_c]) / (
                            points[index_b] - points[index_c]
                        )
    return along_xi, along_eta, node_weight, interp


def two_parts(table):
    table = np.asarray(table, np.float32)
    high = table.astype(BF16)
    low = (table - high.astype(np.float32)).astype(BF16)
    return high, low


def as_right(table):
    high, low = two_parts(table)
    return jnp.asarray(np.concatenate([high, low, high], 0))


def span_factors():
    other = np.arange(HALF)[None, :]
    factors = []
    for own in (16 * np.arange(HALF // 16)[:, None], np.arange(16)[:, None]):
        angle = 2.0 * np.pi * ((own * other) % PLANES) / PLANES
        factors += [jnp.asarray(np.cos(angle), F32), jnp.asarray(np.sin(angle), F32)]
    return factors


def granted(mebibytes):
    return pltpu.CompilerParams(vmem_limit_bytes=mebibytes * 1024 * 1024)


def split(value):
    high = value.astype(BF16)
    low = (value - high.astype(F32)).astype(BF16)
    return high, low


def dot(left, right):
    return jnp.dot(left, right, preferred_element_type=F32)


def left_split(value):
    high, low = split(value)
    return jnp.concatenate([high, high, low], -1)


def twice_high(table):
    return jnp.concatenate([table, table[:, : table.shape[1] // 2]], 1)


def right_split(value):
    high, low = split(value)
    return jnp.concatenate([high, high, low], 0)


def lane_scalars(first, second):
    lane = lax.broadcasted_iota(jnp.int32, (1, LANES), 1)
    return jnp.where(lane < LANES // 2, first, second)


def pack_kernel(field_ref, out_ref):
    for block in range(out_ref.shape[0]):
        out_ref[block] = field_ref[:, pl.ds(block * LANES, LANES)]


def pack(field):
    step = 8
    return pl.pallas_call(
        pack_kernel,
        grid=(GROUPS // step,),
        in_specs=[pl.BlockSpec((ROWS, step * LANES), lambda i: (0, i))],
        out_specs=pl.BlockSpec((step, ROWS, LANES), lambda i: (i, 0, 0)),
        out_shape=jax.ShapeDtypeStruct((GROUPS, ROWS, LANES), F32),
        compiler_params=granted(60),
        cost_estimate=pl.CostEstimate(flops=0, bytes_accessed=1600000, transcendentals=0),
        name="pack",
    )(field)


def trace_kernel(rotor_ref, packed_ref, out_ref, top_ref):
    lane = lax.broadcasted_iota(jnp.int32, (ROWS, LANES), 1)
    zeros = jnp.zeros((LANES - ROWS, LANES), F32)
    for half in range(2):
        rows = jnp.zeros((ROWS, LANES), F32)
        for block in range(8):
            field = packed_ref[half * 8 + block]
            low = pltpu.roll(field, (16 * block - 56) % LANES, 1)
            high = pltpu.roll(field, (16 * block + 8 - 120) % LANES, 1)
            rows = jnp.where(lane // 8 == 2 * block, low, rows)
            rows = jnp.where(lane // 8 == 2 * block + 1, high, rows)
        top_ref[pl.ds(half * LANES, LANES), :] = jnp.concatenate([rows, zeros], 0).T
    for slot in range(32):
        start = pl.multiple_of(rotor_ref[slot] * 8, 8)
        out_ref[pl.ds(slot * 8, 8), :] = top_ref[pl.ds(start, 8), :]


def traces(rotor_element, packed):
    return pl.pallas_call(
        trace_kernel,
        in_specs=[pl.BlockSpec(memory_space=SMEM), pl.BlockSpec(memory_space=VMEM)],
        out_specs=pl.BlockSpec(memory_space=VMEM),
        out_shape=jax.ShapeDtypeStruct((256, LANES), F32),
        scratch_shapes=[pltpu.VMEM((256, LANES), F32)],
        compiler_params=granted(4),
        cost_estimate=pl.CostEstimate(flops=0, bytes_accessed=8000000, transcendentals=0),
        name="traces",
    )(rotor_element, packed)


def pair_kernel(mine_ref, other_ref, out_ref):
    out_ref[pl.ds(0, 256), :] = mine_ref[...]
    out_ref[pl.ds(256, 256), :] = other_ref[...]


def pair(mine, other):
    whole = pl.BlockSpec(memory_space=VMEM)
    return pl.pallas_call(
        pair_kernel,
        in_specs=[whole, whole],
        out_specs=whole,
        out_shape=jax.ShapeDtypeStruct((512, LANES), F32),
        compiler_params=granted(2),
        cost_estimate=pl.CostEstimate(flops=0, bytes_accessed=1000000, transcendentals=0),
        name="pair",
    )(mine, other)


def moves(distance, cores=(0, 1)):
    return [
        (2 * z + c, 2 * ((z + (distance if c == 0 else -distance)) % RING) + c)
        for z in range(RING)
        for c in cores
    ]


ACROSS = [(i, i ^ 1) for i in range(2 * RING)]


def helm_kernel(
    metric_ref, area_ref, stator_ref, packed_ref, visc_ref, weight_ref, forward_ref, back_ref, out_ref,
    count_ref,
):
    step = packed_ref.shape[0]
    first = pl.program_id(0) * step

    @pl.when(pl.program_id(0) == 0)
    def _():
        for element in range(32):
            count_ref[element] = 0
        for edge in range(32):
            count_ref[stator_ref[edge]] = count_ref[stator_ref[edge]] + 1

    four = lax.axis_index("four")
    row = lax.broadcasted_iota(jnp.int32, (ROWS, LANES), 0)
    inner = row % 32
    number = jnp.where((inner == 1) & (four == 0), MODES // 2, four * 16 + inner // 2)
    wave = number.astype(F32) / KZ_DIV
    wave_sq = wave * wave
    lane = lax.broadcasted_iota(jnp.int32, (1, LANES), 1)
    bottom = lane % 64 < NQ
    field = packed_ref[...].reshape(step * ROWS, LANES)
    grads = dot(left_split(field), forward_ref[...])
    masses, fluxes = [], []
    for block in range(step):
        pair = (first + block) * 2
        rx, ry, sx, sy = [
            lane_scalars(metric_ref[i, pair], metric_ref[i, pair + 1]) for i in range(4)
        ]
        count = lane_scalars(count_ref[pair], count_ref[pair + 1]).astype(F32)
        own = jnp.where(bottom, TAU_COEF * count, 0.0)
        area = lane_scalars(area_ref[pair], area_ref[pair + 1])
        weight = area * weight_ref[...]
        viscous = weight * visc_ref[pl.ds(first + block, 1), :]
        rows = slice(block * ROWS, (block + 1) * ROWS)
        grad_xi, grad_eta = grads[rows, :LANES], grads[rows, LANES:]
        cross = viscous * (rx * sx + ry * sy)
        flux_xi = (viscous * (rx * rx + ry * ry)) * grad_xi + cross * grad_eta
        flux_eta = cross * grad_xi + (viscous * (sx * sx + sy * sy)) * grad_eta
        fluxes.append(jnp.concatenate([flux_xi, flux_eta], 1))
        masses.append((weight * LAMBDA_COEF + own + viscous * wave_sq) * field[rows])
    stiff = dot(left_split(jnp.concatenate(fluxes, 0)), back_ref[...])
    for block in range(step):
        out_ref[block] = masses[block] + stiff[block * ROWS : (block + 1) * ROWS]


def helmholtz(metric, area, stator_element, packed, visc, weight, forward, back):
    step = 4
    return pl.pallas_call(
        helm_kernel,
        grid=(GROUPS // step,),
        in_specs=[
            pl.BlockSpec(memory_space=SMEM),
            pl.BlockSpec(memory_space=SMEM),
            pl.BlockSpec(memory_space=SMEM),
            pl.BlockSpec((step, ROWS, LANES), lambda i: (i, 0, 0)),
            pl.BlockSpec((GROUPS, LANES), lambda i: (0, 0)),
            pl.BlockSpec((1, LANES), lambda i: (0, 0)),
            pl.BlockSpec((3 * LANES, 2 * LANES), lambda i: (0, 0)),
            pl.BlockSpec((6 * LANES, LANES), lambda i: (0, 0)),
        ],
        out_specs=pl.BlockSpec((step, ROWS, LANES), lambda i: (i, 0, 0)),
        out_shape=jax.ShapeDtypeStruct((GROUPS, ROWS, LANES), F32),
        scratch_shapes=[pltpu.SMEM((32,), jnp.int32)],
        compiler_params=granted(8),
        cost_estimate=pl.CostEstimate(flops=2000000000, bytes_accessed=8000000, transcendentals=0),
        name="helm",
    )(metric, area, stator_element, packed, visc, weight, forward, back)


def make_tables(back, factors, table_ref):
    count, width = (PAIRS, HALF) if back else (HALF, PAIRS)
    cos_far_ref, sin_far_ref, cos_near_ref, sin_near_ref = factors
    near_cos, near_sin = cos_near_ref[:, pl.ds(0, width)], sin_near_ref[:, pl.ds(0, width)]
    row = lax.broadcasted_iota(jnp.int32, (16, width), 0)
    for step in range(count // 16):
        far_cos = cos_far_ref[pl.ds(step, 1), pl.ds(0, width)]
        far_sin = sin_far_ref[pl.ds(step, 1), pl.ds(0, width)]
        cosine = far_cos * near_cos - far_sin * near_sin
        sine = far_sin * near_cos + far_cos * near_sin
        if back:
            half = (row == 0) & (step == 0)
            cosine = jnp.where(half, 1.0 / PLANES, 2.0 / PLANES) * cosine
            sine = (2.0 / PLANES) * sine
        rows = pl.ds((HALF if back else 0) + step * 16, 16)
        for index, part in enumerate(split(cosine) + split(sine)):
            table_ref[rows, pl.ds(index * width, width)] = part


def plane_kernel(metric_ref, got_ref, forward_ref, *refs):
    factors, (out_ref, table_ref, done_ref, sems) = refs[:4], refs[4:]
    make_tables(False, factors, table_ref)
    pair = lax.axis_index("four") * 2
    rx, ry, sx, sy = [
        lane_scalars(metric_ref[i, pair], metric_ref[i, pair + 1]) for i in range(4)
    ]
    number = lax.broadcasted_iota(jnp.int32, (PAIRS, LANES), 0)
    wave = number.astype(F32) / KZ_DIV
    sign = jnp.where(number % 2 == 0, 1.0, -1.0).astype(F32)
    plane = lax.broadcasted_iota(jnp.int32, (HALF, LANES), 0)
    third = jnp.where(plane % 3 == 0, 1.0, -0.5).astype(F32)
    is_first = plane == 0
    evens, odds = [], []
    for component in range(3):
        start = component * 32
        evens.append(got_ref[:, pl.ds(start, 16, stride=2), :].reshape(PAIRS, LANES))
        odds.append(got_ref[:, pl.ds(start + 1, 16, stride=2), :].reshape(PAIRS, LANES))
    evens_z = [wave * odd for odd in odds]
    odds_z = [-wave * even for even in evens]
    last_cos = [odd[0:1] for odd in odds]
    even_all = jnp.concatenate(evens + evens_z, 1)
    odd_all = jnp.concatenate(odds + odds_z, 1)
    cos_part = dot(twice_high(table_ref[pl.ds(0, HALF), pl.ds(0, 2 * PAIRS)]), right_split(even_all))
    sin_part = dot(twice_high(table_ref[pl.ds(0, HALF), pl.ds(2 * PAIRS, 2 * PAIRS)]), right_split(odd_all))
    make_tables(True, factors, table_ref)
    plus, minus = [], []
    for index in range(6):
        lanes = slice(index * LANES, (index + 1) * LANES)
        cos_here, sin_here = cos_part[:, lanes], sin_part[:, lanes]
        middle = jnp.sum(sign * (evens + evens_z)[index], 0, keepdims=True)
        if index < 3:
            cos_here = cos_here + third * last_cos[index]
            middle = middle + last_cos[index]
        plus.append(cos_here + sin_here)
        minus.append(jnp.where(is_first, middle, cos_here - sin_here))

    speeds = [
        (values[0] * rx + values[1] * ry, values[0] * sx + values[1] * sy, values)
        for values in (plus, minus)
    ]
    cos_back, sin_back = [
        twice_high(table_ref[pl.ds(HALF, PAIRS), pl.ds(start, 2 * HALF)]) for start in (0, 2 * HALF)
    ]
    scale = jnp.where(number == 0, 1.0 / PLANES, 2.0 / PLANES).astype(F32)
    stores = []
    for index, components in enumerate(((0, 1), (2,))):
        even_sum, odd_sum, middles = [], [], []
        for component in components:
            both = []
            for along_xi, along_eta, values in speeds:
                grads = dot(left_split(values[component]), forward_ref[...])
                both.append(
                    along_xi * grads[:, :LANES]
                    + along_eta * grads[:, LANES:]
                    + values[2] * values[3 + component]
                )
            middles.append(both[1][0:1])
            mirrored = jnp.where(is_first, 0.0, both[1])
            even_sum.append(both[0] + mirrored)
            odd_sum.append(both[0] - mirrored)
        even_out = dot(cos_back, right_split(jnp.concatenate(even_sum, 1)))
        odd_out = dot(sin_back, right_split(jnp.concatenate(odd_sum, 1)))
        for i, component in enumerate(components):
            lanes = slice(i * LANES, (i + 1) * LANES)
            even_here = even_out[:, lanes] + (scale * sign) * middles[i]
            last = (2.0 / PLANES) * (
                jnp.sum(third * even_sum[i], 0, keepdims=True) + middles[i]
            )
            odd_here = jnp.where(number == 0, last, odd_out[:, lanes])
            start = component * 32
            done_ref[:, pl.ds(start, 16, stride=2), :] = even_here.reshape(GROUPS, 16, LANES)
            done_ref[:, pl.ds(start + 1, 16, stride=2), :] = odd_here.reshape(GROUPS, 16, LANES)
        rows = pl.ds(components[0] * 32, len(components) * 32)
        store = pltpu.make_async_copy(done_ref.at[:, rows], out_ref.at[:, rows], sems.at[index])
        store.start()
        stores.append(store)
    for store in stores:
        store.wait()


def planes(metric, got, factors, forward):
    whole = pl.BlockSpec(memory_space=VMEM)
    return pl.pallas_call(
        plane_kernel,
        in_specs=[pl.BlockSpec(memory_space=SMEM)] + [whole] * 6,
        out_specs=pl.BlockSpec(memory_space=pl.ANY),
        out_shape=jax.ShapeDtypeStruct((GROUPS, ROWS, LANES), F32),
        scratch_shapes=[
            pltpu.VMEM((HALF + PAIRS, 4 * HALF), BF16),
            pltpu.VMEM((GROUPS, ROWS, LANES), F32),
            pltpu.SemaphoreType.DMA((2,)),
        ],
        compiler_params=granted(20),
        cost_estimate=pl.CostEstimate(flops=3000000000, bytes_accessed=4000000, transcendentals=0),
        name="planes",
    )(metric, got, forward, *factors)


def place_kernel(stator_ref, offset_ref, interp_ref, out_ref, base_ref, place_ref):
    for edge in range(32):
        rows = pl.ds(edge * 8, 8)
        base_ref[rows, :] = interp_ref[pl.ds(pl.multiple_of(offset_ref[edge] * 8, 8), 8), :]
        place_ref[rows, :] = jnp.full((8, 256), stator_ref[edge], jnp.int32)
    lane = lax.broadcasted_iota(jnp.int32, (256, 256), 1)
    high, low = split(jnp.where(place_ref[...] == lane // 8, base_ref[...], 0.0))
    out_ref[...] = jnp.concatenate([high, low, high], 0)


def placing(stator_element, mortar_offset, interp):
    scalars = pl.BlockSpec(memory_space=SMEM)
    whole = pl.BlockSpec(memory_space=VMEM)
    return pl.pallas_call(
        place_kernel,
        in_specs=[scalars, scalars, whole],
        out_specs=whole,
        out_shape=jax.ShapeDtypeStruct((768, 256), BF16),
        scratch_shapes=[pltpu.VMEM((256, 256), F32), pltpu.VMEM((256, 256), jnp.int32)],
        compiler_params=granted(4),
        cost_estimate=pl.CostEstimate(flops=1000, bytes_accessed=1000, transcendentals=0),
        name="placing",
    )(stator_element, mortar_offset, interp)


def penalty_kernel(source_ref, place_ref, *refs):
    piece_refs, (out_ref, received_ref) = refs[:HELD], refs[HELD:]
    elem = lax.axis_index("elem")
    core = elem % 2
    for edge in range(32):
        source = source_ref[edge]
        owner, slot = lax.shift_right_logical(source, 5), source & 31
        owner_core = owner & 1
        behind = (elem // 2 - lax.shift_right_logical(owner, 1)) & (RING - 1)
        near = jnp.where(behind <= 4, behind, RING - behind)
        side = jnp.where(
            behind == 0, core, jnp.where(behind == 4, owner_core, jnp.where(behind < 4, 0, 1))
        )
        piece = jnp.where((behind == 0) | (side == core), near, near + 4)
        first = pl.multiple_of(slot * 8, 8)
        start = pl.multiple_of((jnp.where(side == owner_core, 0, 32) + slot) * 8, 8)
        tile = piece_refs[0][pl.ds(start, 8), :]
        for index in range(1, HELD):
            at = first if index % 4 == 0 else start
            tile = jnp.where(piece == index, piece_refs[index][pl.ds(at, 8), :], tile)
        received_ref[pl.ds(edge * 8, 8), :] = tile
    out_ref[...] = dot(left_split(received_ref[...].T[:ROWS]), place_ref[...])


def penalty(stator_source, place, pieces):
    whole = pl.BlockSpec(memory_space=VMEM)
    return pl.pallas_call(
        penalty_kernel,
        in_specs=[pl.BlockSpec(memory_space=SMEM)] + [whole] * (HELD + 1),
        out_specs=whole,
        out_shape=jax.ShapeDtypeStruct((ROWS, 256), F32),
        scratch_shapes=[pltpu.VMEM((256, LANES), F32)],
        compiler_params=granted(6),
        cost_estimate=pl.CostEstimate(flops=1000, bytes_accessed=1000, transcendentals=0),
        name="penalty",
    )(stator_source, place, *pieces)


def sum_kernel(nonlinear_ref, helm_ref, placed_ref, out_ref, done_ref, sems):
    stores = [
        pltpu.make_async_copy(
            done_ref.at[block], out_ref.at[:, pl.ds(block * LANES, LANES)], sems.at[block]
        )
        for block in range(GROUPS)
    ]
    lane = lax.broadcasted_iota(jnp.int32, (ROWS, LANES), 1)
    for block in range(GROUPS):
        half = placed_ref[:, pl.ds((block // 8) * LANES, LANES)]
        start = 16 * (block % 8)
        low = pltpu.roll(half, (-start) % LANES, 1)
        high = pltpu.roll(half, (64 - 8 - start) % LANES, 1)
        value = jnp.where(lane < 8, low, jnp.where(lane // 8 == 8, high, 0.0))
        done_ref[block] = value - helm_ref[block] - nonlinear_ref[block]
        stores[block].start()
    for store in stores:
        store.wait()


def final_sum(nonlinear, helm, placed):
    whole = pl.BlockSpec(memory_space=VMEM)
    return pl.pallas_call(
        sum_kernel,
        in_specs=[whole] * 3,
        out_specs=pl.BlockSpec(memory_space=pl.ANY),
        out_shape=jax.ShapeDtypeStruct((ROWS, GROUPS * LANES), F32),
        scratch_shapes=[
            pltpu.VMEM((GROUPS, ROWS, LANES), F32),
            pltpu.SemaphoreType.DMA((GROUPS,)),
        ],
        compiler_params=granted(6),
        cost_estimate=pl.CostEstimate(flops=0, bytes_accessed=2400000, transcendentals=0),
        name="final_sum",
    )(nonlinear, helm, placed)


def local(vel_hat, metric, area, visc, rotor_element, stator_element, mortar_offset, stator_source):
    along_xi, along_eta, node_weight, interp = element_tables()
    forward = as_right(np.concatenate([along_xi.T, along_eta.T], 1))
    back = as_right(np.concatenate([along_xi, along_eta], 0))
    weight = jnp.asarray(np.tile(node_weight, 2)[None, :], F32)
    spread = np.tile(TAU_COEF * interp.transpose(0, 2, 1), (1, 1, 32))
    spread = jnp.asarray(spread.reshape(NQ * NQ, 256), F32)

    packed = pack(vel_hat.reshape(ROWS, GROUPS * LANES))
    got = lax.all_to_all(packed, "four", 0, 0, tiled=True)
    mine = traces(rotor_element, packed)
    both = pair(mine, lax.ppermute(mine, "elem", ACROSS))
    one = lax.ppermute(both, "elem", moves(1))
    three = lax.ppermute(both, "elem", moves(3))
    helm = helmholtz(
        metric, area, stator_element, packed, visc.reshape(GROUPS, LANES), weight, forward, back
    )
    place = placing(stator_element, mortar_offset, spread)
    got, helm = lax.optimization_barrier((got, helm))
    one, three = lax.optimization_barrier((one, three))
    advect_hat = planes(metric, got, span_factors(), forward)
    nonlinear = lax.all_to_all(advect_hat, "four", 0, 0, tiled=True)
    two = lax.ppermute(one, "elem", moves(1))
    four = lax.ppermute(three[:256], "elem", moves(1))
    four, place = lax.optimization_barrier((four, place))
    held = [one, two, three, four]
    pieces = [both] + held + [lax.ppermute(piece, "elem", ACROSS) for piece in held]
    placed = penalty(stator_source, place, pieces)
    return final_sum(nonlinear, helm, placed).reshape(vel_hat.shape)


def solution(mesh):
    in_specs = (
        P(None, "four", "elem"),
        P(None, "elem"),
        P("elem"),
        P("elem"),
        P("elem"),
        P("elem"),
        P("elem"),
        P("elem"),
    )
    out_specs = P(None, "four", "elem")
    return jax.shard_map(local, mesh=mesh, in_specs=in_specs, out_specs=out_specs, check_vma=False)
```
